256 devices in a mesh: row: 16 (over x, z_hi), col: 16 (over z_lo, y, core).
Axes of the slice: x: 4, y: 4, z: 8 (z_hi: 4, z_lo: 2; z = z_hi * 2 + z_lo), core: 2. Of those that a mesh axis runs over, the one named last changes fastest.
Arguments:
- src_embed: bfloat16 [64, 32768], P(None, ('row', 'col')), may hold values from -6.5 to 6.5, as said below
- tgt_embed: bfloat16 [64, 32768], P(None, ('row', 'col')), may hold values from -6.5 to 6.5, as said below
- src_weight: bfloat16 [32768], P(('row', 'col')), may hold values from 0.5 to 2
- tgt_weight: bfloat16 [32768], P(('row', 'col')), may hold values from 0.5 to 2
Outputs:
- src_potential: float32 [32768], P(('row', 'col'))
- tgt_potential: float32 [32768], P(('row', 'col'))
- marginal_error: float32 [], replicated
The draws below stay inside these ranges and needn't reach their ends.
Inputs may be any that keep to these rules, and one draw needn't show every extreme that they name: `src_embed`: entries are real-valued embedding coordinates. `tgt_embed`: entries are real-valued embedding coordinates.
All inputs are finite; a program needn't handle non-finite values.
Results may differ from the reference program's by a relative error of at most 0.0003.
Values may be sent and summed in bfloat16 or wider, within the bound.
No kernel may reach another device: no remote copies, remote signals or barrier semaphores. Data moves between devices by JAX's collectives and lax.ppermute only.
A program may use at most 64 MiB of HBM per device.

```python
import math
import jax
import jax.numpy as jnp
from jax import lax

E = 64
ITERS = 3
M = 32768
N = 32768


def base_field(key, width):
    return jnp.clip(jax.random.normal(key, (E, width), jnp.float32), -6.0, 6.0)


def own_field(key, width):
    return jnp.clip(jax.random.normal(key, (E, width), jnp.float32), -6.0, 6.0)


def draw_src_embed(key, part):
    common = base_field(key, M)
    key = jax.random.fold_in(key, 11)
    field = own_field(key, M)
    column = jnp.arange(M)
    strength = 3.5 + 0.5 * (column % 3).astype(jnp.float32)
    signs = jnp.where(common >= 0.0, 1.0, -1.0)
    distant = strength[None, :] * signs
    field = jnp.where((column % 251 == 3)[None, :], distant, field)
    return field.astype(jnp.bfloat16)


def draw_tgt_embed(key, part):
    key = jax.random.fold_in(key, 23)
    field = own_field(key, N)
    return field.astype(jnp.bfloat16)


def block_levels(rng, extent, split, low, high):
    factor_of = 1.0
    for position, blocks in split:
        steps = jax.random.uniform(jax.random.fold_in(jax.random.fold_in(rng, 6), position), (blocks,), jnp.float32, low / len(split), high / len(split))
        factor_of = factor_of * jnp.repeat(jnp.exp(steps), extent[position] // blocks).reshape((-1,) + (1,) * (len(extent) - 1 - position))
    return factor_of


def setup_inputs(seed: int = 0) -> dict:
    keys = jax.random.split(jax.random.key(seed), 5)
    return {
        "src_embed": draw_src_embed(jax.random.fold_in(keys[4], 71), 0),
        "tgt_embed": draw_tgt_embed(jax.random.fold_in(keys[4], 71), 0),
        "src_weight": jnp.clip(jnp.exp(math.log(2.0) - 1.3862944 * jax.random.uniform(keys[2], (M,), jnp.float32) ** block_levels(keys[2], (M,), ((0, 256),), -0.2, 0.2)), 0.5, 2.0).astype(jnp.bfloat16),
        "tgt_weight": jnp.clip(jnp.exp(math.log(2.0) - 1.3862944 * jax.random.uniform(keys[3], (N,), jnp.float32) ** block_levels(keys[3], (N,), ((0, 256),), -0.2, 0.2)), 0.5, 2.0).astype(jnp.bfloat16),
    }


EPS = 0.02

def lse_rows(a_embed, a_norm, a_weight, b_embed, b_norm, b_weight, b_pot):
    rows = a_embed.shape[1]
    block = min(1024, rows)
    count = rows // block
    embeds = a_embed.reshape(a_embed.shape[0], count, block).transpose(1, 0, 2)
    norms = a_norm.reshape(count, block)
    weights = a_weight.reshape(count, block)

    def one(items):
        embed, norm, weight = items
        inner = lax.dot_general(embed, b_embed, (((0,), (0,)), ((), ())), preferred_element_type=jnp.float32)
        cost = weight[:, None] * b_weight[None, :] * (norm[:, None] + b_norm[None, :] - 2.0 * inner) / E
        score = (b_pot[None, :] - cost) / EPS
        top = lax.optimization_barrier(jnp.max(score, axis=1))
        return top + jnp.log(lax.optimization_barrier(jnp.sum(jnp.exp(score - top[:, None]), axis=1)))
    return lax.map(one, (embeds, norms, weights)).reshape(rows)

def reference(src_embed, tgt_embed, src_weight, tgt_weight):
    src_norm = lax.optimization_barrier(jnp.sum(src_embed.astype(jnp.float32) ** 2, axis=0))
    tgt_norm = lax.optimization_barrier(jnp.sum(tgt_embed.astype(jnp.float32) ** 2, axis=0))
    src_w = src_weight.astype(jnp.float32)
    tgt_w = tgt_weight.astype(jnp.float32)
    src_shift = EPS * jnp.log(jnp.float32(M))
    tgt_shift = EPS * jnp.log(jnp.float32(N))
    tgt_pot = jnp.zeros((N,), jnp.float32)
    src_pot = jnp.zeros((M,), jnp.float32)
    for step in range(ITERS):
        src_pot = -EPS * lse_rows(src_embed, src_norm, src_w, tgt_embed, tgt_norm, tgt_w, tgt_pot) - src_shift
        tgt_pot = -EPS * lse_rows(tgt_embed, tgt_norm, tgt_w, src_embed, src_norm, src_w, src_pot) - tgt_shift
    check = -EPS * lse_rows(src_embed, src_norm, src_w, tgt_embed, tgt_norm, tgt_w, tgt_pot) - src_shift
    diff = (src_pot - check) / EPS
    error = jnp.sqrt(jnp.sum(diff * diff) / M)
    return (src_pot, tgt_pot, error)
```

```python
import functools
import math

import jax
import jax.numpy as jnp
from jax import lax
from jax.experimental import pallas as pl
from jax.experimental.pallas import tpu as pltpu
from jax.sharding import Mesh, PartitionSpec as P

EPS = 0.02
ITERS = 3
LANES = 128
TAIL = 16
PACK = 16
UNIT = 1.0 / (EPS * math.log(2.0))
AXES = ("x", "zh", "zl", "y", "c")
SRC_GROUP = ("x", "y")
TGT_GROUP = ("zh", "zl", "c")

f32 = jnp.float32
bf16 = jnp.bfloat16


def log2(value):
    return jnp.log(value) * (1.0 / math.log(2.0))


def pieces(value):
    high = value.astype(bf16).astype(f32)
    rest = value - high
    middle = rest.astype(bf16).astype(f32)
    low = (rest - middle).astype(bf16).astype(f32)
    return high, middle, low


def stack(rows, width):
    index = lax.broadcasted_iota(jnp.int32, (TAIL, width), 0)
    out = jnp.zeros((TAIL, width), f32)
    for place, row in rows:
        out = jnp.where(index == place, row, out)
    return out


def prepare(cells_ref, wide_ref, tail_ref, raw_ref, scale_ref):
    depth = raw_ref.shape[0]
    for b in range(cells_ref.shape[0]):
        at = pl.ds(b * LANES, LANES)
        embed = cells_ref[b, :depth, :]
        raw_ref[:, at] = embed
        value = embed.astype(f32)
        weight = cells_ref[b, depth : depth + PACK, :].astype(f32)[0:1]
        norm = jnp.sum(value * value, axis=0, keepdims=True)
        scale_ref[b : b + 1, :] = weight * (UNIT / depth)
        scaled = (2.0 * weight) * value
        high = scaled.astype(bf16).astype(f32)
        low = scaled - high
        one = jnp.ones_like(weight)
        n = pieces(norm)
        wn = pieces(weight * norm)
        tail_ref[:, at] = stack([(0, one), (1, one), (2, one), (3, n[0]), (4, n[1]), (5, n[2])], LANES)
        tail = stack(
            [(0, -wn[0]), (1, -wn[1]), (2, -wn[2])]
            + [(3, -weight), (4, -weight), (5, -weight), (6, one), (7, one), (8, one)],
            LANES,
        )
        wide_ref[at, :] = jnp.concatenate([high, low, tail], axis=0).T.astype(bf16)


def block_pass(wide_ref, raw_ref, tail_ref, scale_ref, summed, kept, rows_ref, part_ref, with_top):
    size = raw_ref.shape[1]
    width = 2 * LANES
    if summed is not None:
        column = summed.T
        for b in range(wide_ref.shape[0] // LANES):
            rows_ref[pl.ds(b * LANES, LANES), :] = jnp.broadcast_to(column[:, b : b + 1], (LANES, LANES))
    if kept is not None:
        ratio = pieces(kept / scale_ref[...])
    for s in range(size // width):
        at = pl.ds(s * width, width)

        def row(array):
            return jnp.concatenate([array[2 * s : 2 * s + 1, :], array[2 * s + 1 : 2 * s + 2, :]], axis=1)

        tail = tail_ref[:, at]
        if kept is not None:
            tail = tail + stack([(6, row(ratio[0])), (7, row(ratio[1])), (8, row(ratio[2]))], width)
        raw = raw_ref[:, at]
        operand = jnp.concatenate([raw, raw, tail.astype(bf16)], axis=0)
        score = jnp.dot(wide_ref[...], operand, preferred_element_type=f32)
        score = score * row(scale_ref)
        if summed is not None:
            score = score + jnp.concatenate([rows_ref[...], rows_ref[...]], axis=1)
        if with_top:
            top = jnp.max(score, axis=0, keepdims=True)
            score = score - top
            part_ref[1, 2 * s : 2 * s + 1, :] = top[:, :LANES]
            part_ref[1, 2 * s + 1 : 2 * s + 2, :] = top[:, LANES:]
        mass = jnp.sum(jnp.exp2(score), axis=0, keepdims=True)
        part_ref[0, 2 * s : 2 * s + 1, :] = mass[:, :LANES]
        part_ref[0, 2 * s + 1 : 2 * s + 2, :] = mass[:, LANES:]


def combine_tops(got_ref, shift):
    top = jnp.max(got_ref[:, 1], axis=0)
    mass = jnp.sum(got_ref[:, 0] * jnp.exp2(got_ref[:, 1] - top[None]), axis=0)
    return -(top + log2(mass)) - shift


def combine(got_ref, old, shift):
    return old - log2(jnp.sum(got_ref[:, 0], axis=0)) - shift


def send(part_ref, out_ref):
    out_ref[...] = jnp.broadcast_to(part_ref[...][None], out_ref.shape)


def first_kernel(src, tgt, s_wide, s_tail, s_raw, s_scale, t_wide, t_tail, t_raw, t_scale, out, part):
    prepare(src, s_wide, s_tail, s_raw, s_scale)
    prepare(tgt, t_wide, t_tail, t_raw, t_scale)
    block_pass(t_wide, s_raw, s_tail, s_scale, None, None, None, part, True)
    send(part, out)


def second_kernel(shift, got, wide, raw, tail, scale, new, out, rows, part):
    new[...] = combine_tops(got, shift)
    block_pass(wide, raw, tail, scale, new[...], None, rows, part, True)
    send(part, out)


def third_kernel(shift, got, kept, wide, raw, tail, scale, new, out, rows, part):
    new[...] = combine_tops(got, shift)
    block_pass(wide, raw, tail, scale, new[...], kept[...], rows, part, False)
    send(part, out)


def later_kernel(shift, got, old, kept, wide, raw, tail, scale, new, out, rows, part):
    new[...] = combine(got, old[...], shift)
    block_pass(wide, raw, tail, scale, new[...], kept[...], rows, part, False)
    send(part, out)


def last_kernel(shift, got, out):
    diff = (log2(jnp.sum(got[:, 0], axis=0)) + shift) * math.log(2.0)
    out[...] = jnp.full(out.shape, jnp.sum(diff * diff), f32)


def call(kernel, args, outs, scratch, name):
    return pl.pallas_call(
        kernel,
        out_shape=[jax.ShapeDtypeStruct(shape, dtype) for shape, dtype in outs],
        in_specs=[pl.BlockSpec(memory_space=pltpu.VMEM)] * len(args),
        out_specs=[pl.BlockSpec(memory_space=pltpu.VMEM)] * len(outs),
        scratch_shapes=scratch,
        compiler_params=pltpu.CompilerParams(vmem_limit_bytes=48 * 1024 * 1024),
        name=name,
    )(*args)


def gather(array, group):
    count = lax.axis_size(group)
    return lax.all_to_all(jnp.broadcast_to(array[None], (count,) + array.shape), group, 0, 0)


def on_device(src_embed, tgt_embed, src_weight, tgt_weight):
    depth, per_dev = src_embed.shape
    src_count, tgt_count = lax.axis_size(SRC_GROUP), lax.axis_size(TGT_GROUP)
    total = per_dev * src_count * tgt_count
    shift = math.log2(total)
    src_size, tgt_size = per_dev * src_count, per_dev * tgt_count
    src_rows, tgt_rows = (src_count, per_dev), (tgt_count, per_dev)

    def packed(embed, weight):
        return jnp.concatenate([embed, jnp.broadcast_to(weight[None], (PACK, per_dev))], axis=0)

    src = gather(packed(src_embed, src_weight), SRC_GROUP)
    tgt = gather(packed(tgt_embed, tgt_weight), TGT_GROUP)

    wide = 2 * depth + TAIL
    operands = []
    for size, rows in ((src_size, src_rows), (tgt_size, tgt_rows)):
        operands += [((size, wide), bf16), ((TAIL, size), f32), ((depth, size), bf16), (rows, f32)]

    def row_out(tops):
        return ((src_count, tops) + src_rows, f32), pltpu.VMEM((tops,) + src_rows, f32)

    def col_out(tops):
        return ((tgt_count, tops) + tgt_rows, f32), pltpu.VMEM((tops,) + tgt_rows, f32)

    out, part = row_out(2)
    s_wide, s_tail, s_raw, s_scale, t_wide, t_tail, t_raw, t_scale, sent = call(
        first_kernel, [src, tgt], operands + [out], [part], "row_pass_1"
    )
    got = gather_parts(sent, SRC_GROUP)
    src_spread = pltpu.VMEM((src_size, LANES), f32)
    tgt_spread = pltpu.VMEM((tgt_size, LANES), f32)
    keep_tgt = [t_raw, t_tail, t_scale]
    keep_src = [s_raw, s_tail, s_scale]

    out, part = col_out(2)
    f, sent = call(
        functools.partial(second_kernel, shift),
        [got, s_wide] + keep_tgt,
        [(src_rows, f32), out],
        [src_spread, part],
        "col_pass_1",
    )
    got = gather_parts(sent, TGT_GROUP)
    out, part = row_out(1)
    g, sent = call(
        functools.partial(third_kernel, shift),
        [got, f, t_wide] + keep_src,
        [(tgt_rows, f32), out],
        [tgt_spread, part],
        "row_pass_2",
    )
    for step in range(2, ITERS + 1):
        got = gather_parts(sent, SRC_GROUP)
        out, part = col_out(1)
        f, sent = call(
            functools.partial(later_kernel, shift),
            [got, f, g, s_wide] + keep_tgt,
            [(src_rows, f32), out],
            [src_spread, part],
            f"col_pass_{step}",
        )
        got = gather_parts(sent, TGT_GROUP)
        out, part = row_out(1)
        g, sent = call(
            functools.partial(later_kernel, shift),
            [got, g, f, t_wide] + keep_src,
            [(tgt_rows, f32), out],
            [tgt_spread, part],
            f"row_pass_{step + 1}",
        )
    got = gather_parts(sent, SRC_GROUP)
    (sent,) = call(
        functools.partial(last_kernel, shift), [got], [((tgt_count, 8, LANES), f32)], [], "mismatch"
    )
    squares = jnp.sum(gather_parts(sent, TGT_GROUP)[:, 0, 0])
    error = jnp.sqrt(squares / total)
    own_src = lax.dynamic_index_in_dim(f, lax.axis_index(SRC_GROUP), 0, False) * (1.0 / UNIT)
    own_tgt = lax.dynamic_index_in_dim(g, lax.axis_index(TGT_GROUP), 0, False) * (1.0 / UNIT)
    return own_src, own_tgt, error


def gather_parts(sent, group):
    return lax.all_to_all(sent, group, 0, 0)


def solution(mesh, shape=(4, 4, 2, 4, 2)):
    placed = Mesh(mesh.devices.reshape(shape), AXES)
    return jax.shard_map(
        on_device,
        mesh=placed,
        in_specs=(P(None, AXES), P(None, AXES), P(AXES), P(AXES)),
        out_specs=(P(AXES), P(AXES), P()),
        check_vma=False,
    )
```

```python
import functools
import math

import jax
import jax.numpy as jnp
from jax import lax
from jax.experimental import pallas as pl
from jax.experimental.pallas import tpu as pltpu
from jax.sharding import Mesh, PartitionSpec as P

EPS = 0.02
ITERS = 3
LANES = 128
TAIL = 16
PACK = 16
WIDTH = 2 * LANES
HEAD = 512
MARGIN = 80.0
LARGE = 2.0**120
UNIT = 1.0 / (EPS * math.log(2.0))
AXES = ("x", "zh", "zl", "y", "c")
SRC_GROUP = ("x", "y")
TGT_GROUP = ("zh", "zl", "c")

f32 = jnp.float32
bf16 = jnp.bfloat16


def log2(value):
    return jnp.log(value) * (1.0 / math.log(2.0))


def pieces(value):
    high = value.astype(bf16).astype(f32)
    rest = value - high
    middle = rest.astype(bf16).astype(f32)
    low = (rest - middle).astype(bf16).astype(f32)
    return high, middle, low


def stack(rows, width):
    index = lax.broadcasted_iota(jnp.int32, (TAIL, width), 0)
    out = jnp.zeros((TAIL, width), f32)
    for place, row in rows:
        out = jnp.where(index == place, row, out)
    return out


def prepare(blocks, wide_ref, tail_ref, raw_ref, scale_ref):
    depth = raw_ref.shape[0]
    for cells, place in blocks:
        at = pl.ds(pl.multiple_of(place * LANES, LANES), LANES)
        embed = cells[:depth, :]
        raw_ref[:, at] = embed
        value = embed.astype(f32)
        weight = cells[depth : depth + PACK, :].astype(f32)[0:1]
        norm = jnp.sum(value * value, axis=0, keepdims=True)
        scale_ref[pl.ds(place, 1), :] = weight * (UNIT / depth)
        scaled = (2.0 * weight) * value
        high = scaled.astype(bf16).astype(f32)
        low = scaled - high
        one = jnp.ones_like(weight)
        n = pieces(norm)
        wn = pieces(weight * norm)
        tail_ref[:, at] = stack([(0, one), (1, one), (2, one), (3, n[0]), (4, n[1]), (5, n[2])], LANES)
        tail = stack(
            [(0, -wn[0]), (1, -wn[1]), (2, -wn[2])]
            + [(3, -weight), (4, -weight), (5, -weight), (6, one), (7, one), (8, one)],
            LANES,
        )
        wide_ref[at, :] = jnp.concatenate([high, low, tail], axis=0).T.astype(bf16)


def spread(summed, rows_ref):
    column = summed.T
    for b in range(rows_ref.shape[0] // LANES):
        rows_ref[pl.ds(b * LANES, LANES), :] = jnp.broadcast_to(column[:, b : b + 1], (LANES, LANES))


def strip_score(s, wide_ref, raw_ref, tail_ref, scale_ref, ratio, rows_ref):
    at = pl.ds(s * WIDTH, WIDTH) if isinstance(s, int) else pl.ds(pl.multiple_of(s * WIDTH, WIDTH), WIDTH)

    def row(array):
        return jnp.concatenate([array[pl.ds(2 * s, 1), :], array[pl.ds(2 * s + 1, 1), :]], axis=1)

    tail = tail_ref[:, at]
    if ratio is not None:
        parts = [jnp.concatenate([p[2 * s : 2 * s + 1], p[2 * s + 1 : 2 * s + 2]], axis=1) for p in ratio]
        tail = tail + stack([(6, parts[0]), (7, parts[1]), (8, parts[2])], WIDTH)
    raw = raw_ref[:, at]
    operand = jnp.concatenate([raw, raw, tail.astype(bf16)], axis=0)
    score = jnp.dot(wide_ref[...], operand, preferred_element_type=f32) * row(scale_ref)
    if rows_ref is not None:
        score = score + jnp.concatenate([rows_ref[...], rows_ref[...]], axis=1)
    return score


def put(ref, s, value):
    ref[pl.ds(2 * s, 1), :] = value[:, :LANES]
    ref[pl.ds(2 * s + 1, 1), :] = value[:, LANES:]


def sum_pass(operands, rows_ref, kept, part_ref):
    ratio = pieces(kept / operands[3][...])
    for s in range(part_ref.shape[0] // 2):
        score = strip_score(s, *operands, ratio, rows_ref)
        put(part_ref, s, jnp.sum(jnp.exp2(score), axis=0, keepdims=True))


def log_pass(operands, rows_ref, part_ref, top_ref):
    count = part_ref.shape[0] // 2
    for s in range(count):
        score = strip_score(s, *operands, None, rows_ref)
        top = jnp.max(score[: min(HEAD, score.shape[0])], axis=0, keepdims=True) + MARGIN
        put(top_ref, s, top)
        put(part_ref, s, jnp.sum(jnp.exp2(score - top), axis=0, keepdims=True))

    @pl.when(jnp.logical_not(jnp.max(part_ref[...]) < LARGE))
    def _():
        def again(s, carry):
            score = strip_score(s, *operands, None, rows_ref)
            top = jnp.max(score, axis=0, keepdims=True)
            put(top_ref, s, top)
            put(part_ref, s, jnp.sum(jnp.exp2(score - top), axis=0, keepdims=True))
            return carry

        lax.fori_loop(0, count, again, 0)


def combine_logs(got_ref, shift):
    got = got_ref[...]
    top = jnp.max(got, axis=0)
    return -(top + log2(jnp.sum(jnp.exp2(got - top[None]), axis=0))) - shift


def combine(got_ref, old, shift):
    return old - log2(jnp.sum(got_ref[...], axis=0)) - shift


def send(part, out_ref):
    out_ref[...] = jnp.broadcast_to(part[None], out_ref.shape)


def pack_kernel(src_embed, tgt_embed, src_weight, tgt_weight, src_out, tgt_out, embeds, weights, sems):
    copies = [
        pltpu.make_async_copy(source, target, sems.at[k])
        for k, (source, target) in enumerate(
            [
                (src_embed, embeds.at[0]),
                (tgt_embed, embeds.at[1]),
                (src_weight, weights.at[0]),
                (tgt_weight, weights.at[1]),
            ]
        )
    ]
    for copy in copies:
        copy.start()
    for copy in copies:
        copy.wait()
    for k, out in enumerate((src_out, tgt_out)):
        row = jnp.broadcast_to(weights[k].astype(f32), (PACK, LANES)).astype(bf16)
        send(jnp.concatenate([embeds[k], row], axis=0), out)


def sources_kernel(own, far, wide, tail, raw, scale):
    x, y = lax.axis_index("x"), lax.axis_index("y")
    blocks = []
    for m in range(4):
        for k in range(4):
            ref = (own.at[k] if m == 0 else far.at[m - 1, k])
            blocks.append((ref, (x ^ k) * 4 + (y ^ m)))
    prepare(blocks, wide, tail, raw, scale)


def first_kernel(own, other, s_tail, s_raw, s_scale, t_wide, t_tail, t_raw, t_scale, out, part, top):
    core = lax.axis_index("c")
    blocks = [(own.at[z], 2 * z + core) for z in range(own.shape[0])]
    blocks += [(other.at[z], 2 * z + 1 - core) for z in range(own.shape[0])]
    prepare(blocks, t_wide, t_tail, t_raw, t_scale)
    log_pass((t_wide, s_raw, s_tail, s_scale), None, part, top)
    send(top[...] + log2(part[...]), out)


def second_kernel(shift, got, wide, raw, tail, scale, new, out, rows, part, top):
    new[...] = combine_logs(got, shift)
    spread(new[...], rows)
    log_pass((wide, raw, tail, scale), rows, part, top)
    send(top[...] + log2(part[...]), out)


def third_kernel(shift, got, kept, wide, raw, tail, scale, new, out, rows, part):
    new[...] = combine_logs(got, shift)
    spread(new[...], rows)
    sum_pass((wide, raw, tail, scale), rows, kept[...], part)
    send(part[...], out)


def later_kernel(shift, got, old, kept, wide, raw, tail, scale, new, out, rows, part):
    new[...] = combine(got, old[...], shift)
    spread(new[...], rows)
    sum_pass((wide, raw, tail, scale), rows, kept[...], part)
    send(part[...], out)


def last_kernel(shift, got, f, g, out, own_src, own_tgt):
    diff = (log2(jnp.sum(got[...], axis=0)) + shift) * math.log(2.0)
    out[...] = jnp.full(out.shape, jnp.sum(diff * diff), f32)
    own_src[...] = f[pl.ds(lax.axis_index(SRC_GROUP), 1), :] * (1.0 / UNIT)
    own_tgt[...] = g[pl.ds(lax.axis_index(TGT_GROUP), 1), :] * (1.0 / UNIT)


def call(kernel, args, outs, scratch, name):
    return pl.pallas_call(
        kernel,
        out_shape=[jax.ShapeDtypeStruct(shape, dtype) for shape, dtype in outs],
        in_specs=[pl.BlockSpec(memory_space=pltpu.VMEM)] * len(args),
        out_specs=[pl.BlockSpec(memory_space=pltpu.VMEM)] * len(outs),
        scratch_shapes=scratch,
        compiler_params=pltpu.CompilerParams(vmem_limit_bytes=48 * 1024 * 1024),
        name=name,
    )(*args)


def exchange(sent, group):
    return lax.all_to_all(sent, group, 0, 0)


def on_device(src_embed, tgt_embed, src_weight, tgt_weight):
    depth, per_dev = src_embed.shape
    src_count, tgt_count = lax.axis_size(SRC_GROUP), lax.axis_size(TGT_GROUP)
    total = per_dev * src_count * tgt_count
    shift = math.log2(total)
    src_size, tgt_size = per_dev * src_count, per_dev * tgt_count
    src_rows, tgt_rows = (src_count, per_dev), (tgt_count, per_dev)

    cells = (depth + PACK, per_dev)
    z_count = tgt_count // lax.axis_size("c")
    src_sent, tgt_sent = pl.pallas_call(
        pack_kernel,
        out_shape=[
            jax.ShapeDtypeStruct((1,) + cells, bf16),
            jax.ShapeDtypeStruct((z_count,) + cells, bf16),
        ],
        in_specs=[pl.BlockSpec(memory_space=pl.ANY)] * 4,
        out_specs=[pl.BlockSpec(memory_space=pltpu.VMEM)] * 2,
        scratch_shapes=[
            pltpu.VMEM((2, depth, per_dev), bf16),
            pltpu.VMEM((2, 1, per_dev), bf16),
            pltpu.SemaphoreType.DMA((4,)),
        ],
        name="pack",
    )(src_embed, tgt_embed, src_weight[None], tgt_weight[None])

    def neighbours(array, axis):
        size = lax.axis_size(axis)
        return [lax.ppermute(array, axis, [(i, i ^ k) for i in range(size)]) for k in range(1, size)]

    tgt = exchange(tgt_sent, ("zh", "zl"))
    src = jnp.concatenate([src_sent] + neighbours(src_sent, "x"), axis=0)
    src_far = jnp.stack(neighbours(src, "y"))
    (tgt_other,) = neighbours(tgt, "c")

    wide = 2 * depth + TAIL

    def operands(size, rows):
        return [((size, wide), bf16), ((TAIL, size), f32), ((depth, size), bf16), (rows, f32)]

    row_out = ((src_count,) + src_rows, f32)
    col_out = ((tgt_count,) + tgt_rows, f32)
    row_part = pltpu.VMEM(src_rows, f32)
    col_part = pltpu.VMEM(tgt_rows, f32)

    s_wide, s_tail, s_raw, s_scale = call(
        sources_kernel, [src, src_far], operands(src_size, src_rows), [], "sources"
    )
    t_wide, t_tail, t_raw, t_scale, sent = call(
        first_kernel,
        [tgt, tgt_other, s_tail, s_raw, s_scale],
        operands(tgt_size, tgt_rows) + [row_out],
        [row_part, row_part],
        "row_pass_1",
    )
    got = exchange(sent, SRC_GROUP)
    src_spread = pltpu.VMEM((src_size, LANES), f32)
    tgt_spread = pltpu.VMEM((tgt_size, LANES), f32)
    keep_tgt = [t_raw, t_tail, t_scale]
    keep_src = [s_raw, s_tail, s_scale]

    f, sent = call(
        functools.partial(second_kernel, shift),
        [got, s_wide] + keep_tgt,
        [(src_rows, f32), col_out],
        [src_spread, col_part, col_part],
        "col_pass_1",
    )
    got = exchange(sent, TGT_GROUP)
    g, sent = call(
        functools.partial(third_kernel, shift),
        [got, f, t_wide] + keep_src,
        [(tgt_rows, f32), row_out],
        [tgt_spread, row_part],
        "row_pass_2",
    )
    for step in range(2, ITERS + 1):
        got = exchange(sent, SRC_GROUP)
        f, sent = call(
            functools.partial(later_kernel, shift),
            [got, f, g, s_wide] + keep_tgt,
            [(src_rows, f32), col_out],
            [src_spread, col_part],
            f"col_pass_{step}",
        )
        got = exchange(sent, TGT_GROUP)
        g, sent = call(
            functools.partial(later_kernel, shift),
            [got, g, f, t_wide] + keep_src,
            [(tgt_rows, f32), row_out],
            [tgt_spread, row_part],
            f"row_pass_{step + 1}",
        )
    got = exchange(sent, SRC_GROUP)
    sent, own_src, own_tgt = call(
        functools.partial(last_kernel, shift),
        [got, f, g],
        [((tgt_count, 8, LANES), f32), ((1, per_dev), f32), ((1, per_dev), f32)],
        [],
        "mismatch",
    )
    squares = jnp.sum(exchange(sent, TGT_GROUP)[:, 0, 0])
    return own_src[0], own_tgt[0], jnp.sqrt(squares / total)


def solution(mesh, shape=(4, 4, 2, 4, 2)):
    placed = Mesh(mesh.devices.reshape(shape), AXES)
    return jax.shard_map(
        on_device,
        mesh=placed,
        in_specs=(P(None, AXES), P(None, AXES), P(AXES), P(AXES)),
        out_specs=(P(AXES), P(AXES), P()),
        check_vma=False,
    )
```

```python
import functools
import math

import jax
import jax.numpy as jnp
from jax import lax
from jax.experimental import pallas as pl
from jax.experimental.pallas import tpu as pltpu
from jax.sharding import Mesh, PartitionSpec as P

EPS = 0.02
ITERS = 3
LANES = 128
TAIL = 16
PACK = 16
BLOCKS = 2
WIDTH = BLOCKS * LANES
HEAD = 512
MARGIN = 100.0
REACH = 110.0
LARGE = 2.0**120
SMALL = 2.0**-102
UNIT = 1.0 / (EPS * math.log(2.0))
AXES = ("x", "zh", "zl", "y", "c")
SRC_GROUP = ("x", "y")
TGT_GROUP = ("zh", "zl", "c")

f32 = jnp.float32
bf16 = jnp.bfloat16


def log2(value):
    return jnp.log(value) * (1.0 / math.log(2.0))


def pieces(value):
    high = value.astype(bf16).astype(f32)
    rest = value - high
    middle = rest.astype(bf16).astype(f32)
    low = (rest - middle).astype(bf16).astype(f32)
    return high, middle, low


def stack(rows, width):
    index = lax.broadcasted_iota(jnp.int32, (TAIL, width), 0)
    out = jnp.zeros((TAIL, width), f32)
    for place, row in rows:
        out = jnp.where(index == place, row, out)
    return out


def prepare(blocks, wide_ref, tail_ref, raw_ref, scale_ref):
    depth = raw_ref.shape[0]
    for cells, place in blocks:
        at = pl.ds(pl.multiple_of(place * LANES, LANES), LANES)
        embed = cells[:depth, :]
        raw_ref[:, at] = embed
        value = embed.astype(f32)
        weight = cells[depth : depth + PACK, :].astype(f32)[0:1]
        norm = jnp.sum(value * value, axis=0, keepdims=True)
        scale_ref[pl.ds(place, 1), :] = weight * (UNIT / depth)
        scaled = (2.0 * weight) * value
        high = scaled.astype(bf16).astype(f32)
        low = scaled - high
        one = jnp.ones_like(weight)
        n = pieces(norm)
        wn = pieces(weight * norm)
        tail_ref[:, at] = stack([(0, one), (1, one), (2, one), (3, n[0]), (4, n[1]), (5, n[2])], LANES)
        tail = stack(
            [(0, -wn[0]), (1, -wn[1]), (2, -wn[2])]
            + [(3, -weight), (4, -weight), (5, -weight), (6, one), (7, one), (8, one)],
            LANES,
        )
        wide_ref[at, :] = jnp.concatenate([high, low, tail], axis=0).T.astype(bf16)


def spread(summed, rows_ref):
    column = summed.T
    for b in range(rows_ref.shape[0] // LANES):
        rows_ref[pl.ds(b * LANES, LANES), :] = jnp.broadcast_to(column[:, b : b + 1], (LANES, LANES))


def strip_of(s):
    return pl.ds(s * WIDTH, WIDTH) if isinstance(s, int) else pl.ds(pl.multiple_of(s * WIDTH, WIDTH), WIDTH)


def get(ref, s):
    return jnp.concatenate([ref[pl.ds(BLOCKS * s + k, 1), :] for k in range(BLOCKS)], axis=1)


def put(ref, s, value):
    for k in range(BLOCKS):
        ref[pl.ds(BLOCKS * s + k, 1), :] = value[:, k * LANES : (k + 1) * LANES]


def strip_score(s, count, operands, rows_ref, ratio_ref):
    wide_ref, raw_ref, tail_ref, scale_ref = operands
    at = strip_of(s)
    tail = tail_ref[:, at]
    if ratio_ref is not None:
        tail = tail + stack([(6 + k, get(ratio_ref.at[k], s)) for k in range(3)], WIDTH)
    raw = raw_ref[:, at]
    operand = jnp.concatenate([raw, raw, tail.astype(bf16)], axis=0)
    score = jnp.dot(wide_ref[:count, :], operand, preferred_element_type=f32) * get(scale_ref, s)
    if rows_ref is not None:
        rows = rows_ref[:count, :]
        score = score + jnp.concatenate([rows] * BLOCKS, axis=1)
    return score


def strips(count, body, unroll):
    if unroll:
        for s in range(count):
            body(s)
    else:

        def step(s, carry):
            body(s)
            return carry

        lax.fori_loop(0, count, step, 0)


def find_tops(count, operands, rows_ref, top_ref, unroll=True):
    def body(s):
        put(top_ref, s, jnp.max(strip_score(s, count, operands, rows_ref, None), axis=0, keepdims=True))

    strips(top_ref.shape[0] // BLOCKS, body, unroll)


def sum_pass(operands, rows_ref, kept, ratio_ref, part_ref, unroll=True):
    for k, piece in enumerate(pieces(kept / operands[3][...])):
        ratio_ref[k] = piece

    def body(s):
        score = strip_score(s, operands[0].shape[0], operands, rows_ref, ratio_ref)
        put(part_ref, s, jnp.sum(jnp.exp2(score), axis=0, keepdims=True))

    strips(part_ref.shape[0] // BLOCKS, body, unroll)


def log_pass(operands, rows_ref, ratio_ref, part_ref, top_ref, bound=None):
    size = operands[0].shape[0]
    if bound is None:
        find_tops(min(HEAD, size), operands, rows_ref, top_ref)
        top_ref[...] = top_ref[...] + MARGIN
    else:
        top_ref[...] = jnp.full(top_ref.shape, bound - REACH, f32)
    sum_pass(operands, rows_ref, -top_ref[...], ratio_ref, part_ref)
    mass = part_ref[...]
    sound = (mass < LARGE) & (mass > SMALL)

    @pl.when(jnp.min(sound.astype(f32)) < 0.5)
    def _():
        find_tops(size, operands, rows_ref, top_ref, unroll=False)
        sum_pass(operands, rows_ref, -top_ref[...], ratio_ref, part_ref, unroll=False)


def combine_logs(got_ref, shift):
    got = got_ref[...]
    top = jnp.max(got, axis=0)
    return -(top + log2(jnp.sum(jnp.exp2(got - top[None]), axis=0))) - shift


def combine(got_ref, old, shift):
    return old - log2(jnp.sum(got_ref[...], axis=0)) - shift


def send(part, out_ref):
    out_ref[...] = jnp.broadcast_to(part[None], out_ref.shape)


def pack_kernel(src_embed, tgt_embed, src_weight, tgt_weight, src_out, tgt_out, embeds, weights, sems):
    copies = [
        pltpu.make_async_copy(source, target, sems.at[k])
        for k, (source, target) in enumerate(
            [
                (src_embed, embeds.at[0]),
                (tgt_embed, embeds.at[1]),
                (src_weight, weights.at[0]),
                (tgt_weight, weights.at[1]),
            ]
        )
    ]
    for copy in copies:
        copy.start()
    for copy in copies:
        copy.wait()
    for k, out in enumerate((src_out, tgt_out)):
        row = jnp.broadcast_to(weights[k].astype(f32), (PACK, LANES)).astype(bf16)
        send(jnp.concatenate([embeds[k], row], axis=0), out)


def sources_kernel(own, far, wide, tail, raw, scale):
    x, y = lax.axis_index("x"), lax.axis_index("y")
    blocks = []
    for m in range(4):
        for k in range(4):
            ref = (own.at[k] if m == 0 else far.at[m - 1, k])
            blocks.append((ref, (x ^ k) * 4 + (y ^ m)))
    prepare(blocks, wide, tail, raw, scale)


def first_kernel(own, other, s_tail, s_raw, s_scale, t_wide, t_tail, t_raw, t_scale, out, ratio, part, top):
    core = lax.axis_index("c")
    blocks = [(own.at[z], 2 * z + core) for z in range(own.shape[0])]
    blocks += [(other.at[z], 2 * z + 1 - core) for z in range(own.shape[0])]
    prepare(blocks, t_wide, t_tail, t_raw, t_scale)
    log_pass((t_wide, s_raw, s_tail, s_scale), None, ratio, part, top)
    send(top[...] + log2(part[...]), out)


def second_kernel(shift, got, wide, raw, tail, scale, new, out, rows, ratio, part, top):
    new[...] = combine_logs(got, shift)
    spread(new[...], rows)
    log_pass((wide, raw, tail, scale), rows, ratio, part, top, -shift)
    send(top[...] + log2(part[...]), out)


def third_kernel(shift, got, kept, wide, raw, tail, scale, new, out, rows, ratio, part):
    new[...] = combine_logs(got, shift)
    spread(new[...], rows)
    sum_pass((wide, raw, tail, scale), rows, kept[...], ratio, part)
    send(part[...], out)


def later_kernel(shift, got, old, kept, wide, raw, tail, scale, new, out, rows, ratio, part):
    new[...] = combine(got, old[...], shift)
    spread(new[...], rows)
    sum_pass((wide, raw, tail, scale), rows, kept[...], ratio, part)
    send(part[...], out)


def last_kernel(shift, got, f, g, out, own_src, own_tgt):
    diff = (log2(jnp.sum(got[...], axis=0)) + shift) * math.log(2.0)
    out[...] = jnp.full(out.shape, jnp.sum(diff * diff), f32)
    own_src[...] = f[pl.ds(lax.axis_index(SRC_GROUP), 1), :] * (1.0 / UNIT)
    own_tgt[...] = g[pl.ds(lax.axis_index(TGT_GROUP), 1), :] * (1.0 / UNIT)


def call(kernel, args, outs, scratch, name):
    return pl.pallas_call(
        kernel,
        out_shape=[jax.ShapeDtypeStruct(shape, dtype) for shape, dtype in outs],
        in_specs=[pl.BlockSpec(memory_space=pltpu.VMEM)] * len(args),
        out_specs=[pl.BlockSpec(memory_space=pltpu.VMEM)] * len(outs),
        scratch_shapes=scratch,
        compiler_params=pltpu.CompilerParams(vmem_limit_bytes=48 * 1024 * 1024),
        name=name,
    )(*args)


def exchange(sent, group):
    return lax.all_to_all(sent, group, 0, 0)


def on_device(src_embed, tgt_embed, src_weight, tgt_weight):
    depth, per_dev = src_embed.shape
    src_count, tgt_count = lax.axis_size(SRC_GROUP), lax.axis_size(TGT_GROUP)
    total = per_dev * src_count * tgt_count
    shift = math.log2(total)
    src_size, tgt_size = per_dev * src_count, per_dev * tgt_count
    src_rows, tgt_rows = (src_count, per_dev), (tgt_count, per_dev)

    cells = (depth + PACK, per_dev)
    z_count = tgt_count // lax.axis_size("c")
    src_sent, tgt_sent = pl.pallas_call(
        pack_kernel,
        out_shape=[
            jax.ShapeDtypeStruct((1,) + cells, bf16),
            jax.ShapeDtypeStruct((z_count,) + cells, bf16),
        ],
        in_specs=[pl.BlockSpec(memory_space=pl.ANY)] * 4,
        out_specs=[pl.BlockSpec(memory_space=pltpu.VMEM)] * 2,
        scratch_shapes=[
            pltpu.VMEM((2, depth, per_dev), bf16),
            pltpu.VMEM((2, 1, per_dev), bf16),
            pltpu.SemaphoreType.DMA((4,)),
        ],
        name="pack",
    )(src_embed, tgt_embed, src_weight[None], tgt_weight[None])

    def neighbours(array, axis):
        size = lax.axis_size(axis)
        return [lax.ppermute(array, axis, [(i, i ^ k) for i in range(size)]) for k in range(1, size)]

    tgt = exchange(tgt_sent, ("zh", "zl"))
    src = jnp.concatenate([src_sent] + neighbours(src_sent, "x"), axis=0)
    src_far = jnp.stack(neighbours(src, "y"))
    (tgt_other,) = neighbours(tgt, "c")

    wide = 2 * depth + TAIL

    def operands(size, rows):
        return [((size, wide), bf16), ((TAIL, size), f32), ((depth, size), bf16), (rows, f32)]

    row_out = ((src_count,) + src_rows, f32)
    col_out = ((tgt_count,) + tgt_rows, f32)
    row_part = pltpu.VMEM(src_rows, f32)
    col_part = pltpu.VMEM(tgt_rows, f32)
    row_ratio = pltpu.VMEM((3,) + src_rows, f32)
    col_ratio = pltpu.VMEM((3,) + tgt_rows, f32)

    s_wide, s_tail, s_raw, s_scale = call(
        sources_kernel, [src, src_far], operands(src_size, src_rows), [], "sources"
    )
    t_wide, t_tail, t_raw, t_scale, sent = call(
        first_kernel,
        [tgt, tgt_other, s_tail, s_raw, s_scale],
        operands(tgt_size, tgt_rows) + [row_out],
        [row_ratio, row_part, row_part],
        "row_pass_1",
    )
    got = exchange(sent, SRC_GROUP)
    src_spread = pltpu.VMEM((src_size, LANES), f32)
    tgt_spread = pltpu.VMEM((tgt_size, LANES), f32)
    keep_tgt = [t_raw, t_tail, t_scale]
    keep_src = [s_raw, s_tail, s_scale]

    f, sent = call(
        functools.partial(second_kernel, shift),
        [got, s_wide] + keep_tgt,
        [(src_rows, f32), col_out],
        [src_spread, col_ratio, col_part, col_part],
        "col_pass_1",
    )
    got = exchange(sent, TGT_GROUP)
    g, sent = call(
        functools.partial(third_kernel, shift),
        [got, f, t_wide] + keep_src,
        [(tgt_rows, f32), row_out],
        [tgt_spread, row_ratio, row_part],
        "row_pass_2",
    )
    for step in range(2, ITERS + 1):
        got = exchange(sent, SRC_GROUP)
        f, sent = call(
            functools.partial(later_kernel, shift),
            [got, f, g, s_wide] + keep_tgt,
            [(src_rows, f32), col_out],
            [src_spread, col_ratio, col_part],
            "later_pass",
        )
        got = exchange(sent, TGT_GROUP)
        g, sent = call(
            functools.partial(later_kernel, shift),
            [got, g, f, t_wide] + keep_src,
            [(tgt_rows, f32), row_out],
            [tgt_spread, row_ratio, row_part],
            "later_pass",
        )
    got = exchange(sent, SRC_GROUP)
    sent, own_src, own_tgt = call(
        functools.partial(last_kernel, shift),
        [got, f, g],
        [((tgt_count, 1, LANES), f32), ((1, per_dev), f32), ((1, per_dev), f32)],
        [],
        "mismatch",
    )
    squares = jnp.sum(exchange(sent, TGT_GROUP)[:, 0, 0])
    return own_src[0], own_tgt[0], jnp.sqrt(squares / total)


def solution(mesh, shape=(4, 4, 2, 4, 2)):
    placed = Mesh(mesh.devices.reshape(shape), AXES)
    return jax.shard_map(
        on_device,
        mesh=placed,
        in_specs=(P(None, AXES), P(None, AXES), P(AXES), P(AXES)),
        out_specs=(P(AXES), P(AXES), P()),
        check_vma=False,
    )
```

```python
import functools
import math

import jax
import jax.numpy as jnp
from jax import lax
from jax.experimental import pallas as pl
from jax.experimental.pallas import tpu as pltpu
from jax.sharding import Mesh, PartitionSpec as P

EPS = 0.02
ITERS = 3
LANES = 128
TAIL = 16
PACK = 16
BLOCKS = 2
WIDTH = BLOCKS * LANES
GROUPS = 64
VMEM = 8 * 1024 * 1024
UNIT = 1.0 / (EPS * math.log(2.0))
AXES = ("x", "zh", "zl", "y", "c")
SRC_GROUP = ("x", "y")
TGT_GROUP = ("zh", "zl", "c")

f32 = jnp.float32
bf16 = jnp.bfloat16


def log2(value):
    return jnp.log(value) * (1.0 / math.log(2.0))


def pieces(value):
    high = value.astype(bf16).astype(f32)
    rest = value - high
    middle = rest.astype(bf16).astype(f32)
    low = (rest - middle).astype(bf16).astype(f32)
    return high, middle, low


def stack(rows, width):
    index = lax.broadcasted_iota(jnp.int32, (TAIL, width), 0)
    out = jnp.zeros((TAIL, width), f32)
    for place, row in rows:
        out = jnp.where(index == place, row, out)
    return out


def prepare(blocks, wide_ref, tail_ref, raw_ref, scale_ref):
    depth = raw_ref.shape[0]
    for cells, place in blocks:
        at = pl.ds(pl.multiple_of(place * LANES, LANES), LANES)
        embed = cells[:depth, :]
        raw_ref[:, at] = embed
        value = embed.astype(f32)
        weight = cells[depth : depth + PACK, :].astype(f32)[0:1]
        norm = jnp.sum(value * value, axis=0, keepdims=True)
        scale_ref[pl.ds(place, 1), :] = weight * (UNIT / depth)
        scaled = (2.0 * weight) * value
        high = scaled.astype(bf16).astype(f32)
        low = scaled - high
        one = jnp.ones_like(weight)
        n = pieces(norm)
        wn = pieces(weight * norm)
        tail_ref[:, at] = stack([(0, one), (1, one), (2, one), (3, n[0]), (4, n[1]), (5, n[2])], LANES)
        tail = stack(
            [(0, -wn[0]), (1, -wn[1]), (2, -wn[2])]
            + [(3, -weight), (4, -weight), (5, -weight), (6, one), (7, one), (8, one)],
            LANES,
        )
        wide_ref[at, :] = jnp.concatenate([high, low, tail], axis=0).T.astype(bf16)


def spread(summed, rows_ref):
    column = summed.T
    for b in range(rows_ref.shape[0] // LANES):
        rows_ref[pl.ds(b * LANES, LANES), :] = jnp.broadcast_to(column[:, b : b + 1], (LANES, LANES))


def strip_of(s):
    return pl.ds(s * WIDTH, WIDTH) if isinstance(s, int) else pl.ds(pl.multiple_of(s * WIDTH, WIDTH), WIDTH)


def get(ref, s):
    return jnp.concatenate([ref[pl.ds(BLOCKS * s + k, 1), :] for k in range(BLOCKS)], axis=1)


def put(ref, s, value):
    for k in range(BLOCKS):
        ref[pl.ds(BLOCKS * s + k, 1), :] = value[:, k * LANES : (k + 1) * LANES]


def strip_score(s, count, operands, rows_ref, ratio_ref):
    wide_ref, raw_ref, tail_ref, scale_ref = operands
    at = strip_of(s)
    tail = tail_ref[:, at]
    if ratio_ref is not None:
        tail = tail + stack([(6 + k, get(ratio_ref.at[k], s)) for k in range(3)], WIDTH)
    raw = raw_ref[:, at]
    operand = jnp.concatenate([raw, raw, tail.astype(bf16)], axis=0)
    score = jnp.dot(wide_ref[:count, :], operand, preferred_element_type=f32) * get(scale_ref, s)
    if rows_ref is not None:
        rows = rows_ref[:count, :]
        score = score + jnp.concatenate([rows] * BLOCKS, axis=1)
    return score


def strips(count, body, unroll):
    if unroll:
        for s in range(count):
            body(s)
    else:

        def step(s, carry):
            body(s)
            return carry

        lax.fori_loop(0, count, step, 0)


def find_tops(count, operands, rows_ref, top_ref, unroll=True):
    def body(s):
        put(top_ref, s, jnp.max(strip_score(s, count, operands, rows_ref, None), axis=0, keepdims=True))

    strips(top_ref.shape[0] // BLOCKS, body, unroll)


def sum_pass(operands, rows_ref, kept, ratio_ref, part_ref, terms_ref=None, unroll=True):
    for k, piece in enumerate(pieces(kept / operands[3][...])):
        ratio_ref[k] = piece

    def body(s):
        terms = jnp.exp2(strip_score(s, operands[0].shape[0], operands, rows_ref, ratio_ref))
        if terms_ref is not None:
            terms_ref[:, strip_of(s)] = terms
        put(part_ref, s, jnp.sum(terms, axis=0, keepdims=True))

    strips(part_ref.shape[0] // BLOCKS, body, unroll)


def log_pass(operands, rows_ref, ratio_ref, part_ref, top_ref, head, margin, large, terms_ref=None):
    size = operands[0].shape[0]
    find_tops(min(head, size), operands, rows_ref, top_ref)
    top_ref[...] = top_ref[...] + margin
    sum_pass(operands, rows_ref, -top_ref[...], ratio_ref, part_ref, terms_ref)

    @pl.when(jnp.logical_not(jnp.max(part_ref[...]) < large))
    def _():
        find_tops(size, operands, rows_ref, top_ref, unroll=False)
        sum_pass(operands, rows_ref, -top_ref[...], ratio_ref, part_ref, terms_ref, unroll=False)


def product_pass(terms_ref, factor, rows_ref, part_ref):
    spread(factor, rows_ref)
    size = terms_ref.shape[1]

    def step(g, total):
        for q in range(GROUPS):
            at = pl.ds(pl.multiple_of((g * GROUPS + q) * 8, 8), 8)
            total = total + terms_ref[at, :] * jnp.concatenate([rows_ref[at, :]] * (size // LANES), axis=1)
        return total

    total = lax.fori_loop(0, terms_ref.shape[0] // (8 * GROUPS), step, jnp.zeros((8, size), f32))
    total = jnp.sum(total, axis=0, keepdims=True)
    for b in range(size // LANES):
        part_ref[b : b + 1, :] = total[:, b * LANES : (b + 1) * LANES]


def combine_logs(got_ref, shift):
    got = got_ref[...]
    top = jnp.max(got, axis=0)
    return -(top + log2(jnp.sum(jnp.exp2(got - top[None]), axis=0))) - shift


def combine_sums(got_ref, total):
    return 1.0 / (total * jnp.sum(got_ref[...], axis=0))


def send(part, out_ref):
    out_ref[...] = jnp.broadcast_to(part[None], out_ref.shape)


def pack_kernel(src_embed, tgt_embed, src_weight, tgt_weight, src_out, tgt_out, embeds, weights, sems):
    copies = [
        pltpu.make_async_copy(source, target, sems.at[k])
        for k, (source, target) in enumerate(
            [
                (src_embed, embeds.at[0]),
                (tgt_embed, embeds.at[1]),
                (src_weight, weights.at[0]),
                (tgt_weight, weights.at[1]),
            ]
        )
    ]
    for copy in copies:
        copy.start()
    for copy in copies:
        copy.wait()
    for k, out in enumerate((src_out, tgt_out)):
        row = jnp.broadcast_to(weights[k].astype(f32), (PACK, LANES)).astype(bf16)
        send(jnp.concatenate([embeds[k], row], axis=0), out)


def sources_kernel(own, far, _, wide, tail, raw, scale):
    x, y = lax.axis_index("x"), lax.axis_index("y")
    blocks = []
    for m in range(4):
        for k in range(4):
            ref = (own.at[k] if m == 0 else far.at[m - 1, k])
            blocks.append((ref, (x ^ k) * 4 + (y ^ m)))
    prepare(blocks, wide, tail, raw, scale)


def targets_kernel(own, other, wide, tail, raw, scale):
    core = lax.axis_index("c")
    blocks = [(own.at[z], 2 * z + core) for z in range(own.shape[0])]
    blocks += [(other.at[z], 2 * z + 1 - core) for z in range(own.shape[0])]
    prepare(blocks, wide, tail, raw, scale)


def first_kernel(wide, raw, tail, scale, out, ratio, part, top):
    log_pass((wide, raw, tail, scale), None, ratio, part, top, 512, 100.0, 2.0**120)
    send(top[...] + log2(part[...]), out)


def second_kernel(shift, got, wide, raw, tail, scale, new, part, lse, terms, out, rows, ratio, top):
    new[...] = combine_logs(got, shift)
    spread(new[...], rows)
    log_pass((wide, raw, tail, scale), rows, ratio, part, top, 128, 30.0, 2.0**80, terms)
    lse[...] = top[...] + log2(part[...])
    send(lse[...], out)


def third_kernel(shift, got, kept, lse, mass, wide, raw, tail, scale, new, terms, weight, one, out, rows, ratio, part):
    new[...] = combine_logs(got, shift)
    weight[...] = jnp.exp2(lse[...] + new[...]) / mass[...]
    one[...] = jnp.ones_like(one)
    spread(new[...], rows)
    sum_pass((wide, raw, tail, scale), rows, kept[...], ratio, part, terms)
    send(part[...], out)


def product_kernel(total, got, terms, weight, out, rows, part, factor):
    factor[...] = combine_sums(got, total)
    product_pass(terms, factor[...], rows, part)
    send(part[...] * weight[...], out)


def last_product_kernel(total, got, terms, weight, factor, out, rows, part):
    product_kernel(total, got, terms, weight, out, rows, part, factor)


def last_kernel(shift, got, f, g, f_factor, g_factor, out, own_src, own_tgt):
    f_change = log2(f_factor[...])
    diff = (f_change + log2(jnp.sum(got[...], axis=0)) + shift) * math.log(2.0)
    out[...] = jnp.full(out.shape, jnp.sum(diff * diff), f32)
    at = pl.ds(lax.axis_index(SRC_GROUP), 1)
    own_src[...] = (f[at, :] + log2(f_factor[at, :])) * (1.0 / UNIT)
    at = pl.ds(lax.axis_index(TGT_GROUP), 1)
    own_tgt[...] = (g[at, :] + log2(g_factor[at, :])) * (1.0 / UNIT)


def call(kernel, args, outs, scratch, name):
    return pl.pallas_call(
        kernel,
        out_shape=[jax.ShapeDtypeStruct(shape, dtype) for shape, dtype in outs],
        in_specs=[pl.BlockSpec(memory_space=pltpu.VMEM)] * len(args),
        out_specs=[pl.BlockSpec(memory_space=pltpu.VMEM)] * len(outs),
        scratch_shapes=scratch,
        compiler_params=pltpu.CompilerParams(vmem_limit_bytes=VMEM),
        name=name,
    )(*args)


def exchange(sent, group):
    return lax.all_to_all(sent, group, 0, 0)


def on_device(src_embed, tgt_embed, src_weight, tgt_weight):
    depth, per_dev = src_embed.shape
    src_count, tgt_count = lax.axis_size(SRC_GROUP), lax.axis_size(TGT_GROUP)
    total = per_dev * src_count * tgt_count
    shift = math.log2(total)
    src_size, tgt_size = per_dev * src_count, per_dev * tgt_count
    src_rows, tgt_rows = (src_count, per_dev), (tgt_count, per_dev)

    cells = (depth + PACK, per_dev)
    z_count = tgt_count // lax.axis_size("c")
    src_sent, tgt_sent = pl.pallas_call(
        pack_kernel,
        out_shape=[
            pltpu.VMEM((1,) + cells, bf16),
            pltpu.VMEM((z_count,) + cells, bf16),
        ],
        in_specs=[pl.BlockSpec(memory_space=pl.ANY)] * 4,
        out_specs=[pl.BlockSpec(memory_space=pltpu.VMEM)] * 2,
        scratch_shapes=[
            pltpu.VMEM((2, depth, per_dev), bf16),
            pltpu.VMEM((2, 1, per_dev), bf16),
            pltpu.SemaphoreType.DMA((4,)),
        ],
        name="pack",
    )(src_embed, tgt_embed, src_weight[None], tgt_weight[None])

    def neighbours(array, axis):
        size = lax.axis_size(axis)
        return [lax.ppermute(array, axis, [(i, i ^ k) for i in range(size)]) for k in range(1, size)]

    tgt = exchange(tgt_sent, ("zh", "zl"))
    src = jnp.concatenate([src_sent] + neighbours(src_sent, "x"), axis=0)
    src_far = jnp.stack(neighbours(src, "y"))
    (tgt_other,) = neighbours(tgt, "c")

    wide = 2 * depth + TAIL

    def operands(size, rows):
        return [((size, wide), bf16), ((TAIL, size), f32), ((depth, size), bf16), (rows, f32)]

    row_out = ((src_count,) + src_rows, f32)
    col_out = ((tgt_count,) + tgt_rows, f32)
    row_part = pltpu.VMEM(src_rows, f32)
    col_part = pltpu.VMEM(tgt_rows, f32)
    row_ratio = pltpu.VMEM((3,) + src_rows, f32)
    col_ratio = pltpu.VMEM((3,) + tgt_rows, f32)

    t_wide, t_tail, t_raw, t_scale = call(
        targets_kernel, [tgt, tgt_other], operands(tgt_size, tgt_rows), [], "targets"
    )
    s_wide, s_tail, s_raw, s_scale = call(
        sources_kernel, [src, src_far, t_scale], operands(src_size, src_rows), [], "sources"
    )
    (sent,) = call(
        first_kernel,
        [t_wide, s_raw, s_tail, s_scale],
        [row_out],
        [row_ratio, row_part, row_part],
        "row_pass_1",
    )
    got = exchange(sent, SRC_GROUP)
    src_spread = pltpu.VMEM((src_size, LANES), f32)
    tgt_spread = pltpu.VMEM((tgt_size, LANES), f32)
    keep_tgt = [t_raw, t_tail, t_scale]
    keep_src = [s_raw, s_tail, s_scale]

    f, part, lse, terms, sent = call(
        functools.partial(second_kernel, shift),
        [got, s_wide] + keep_tgt,
        [(src_rows, f32), (tgt_rows, f32), (tgt_rows, f32), ((src_size, tgt_size), f32), col_out],
        [src_spread, col_ratio, col_part],
        "col_pass_1",
    )
    got = exchange(sent, TGT_GROUP)
    g, mate, weight, one, sent = call(
        functools.partial(third_kernel, shift),
        [got, f, lse, part, t_wide] + keep_src,
        [(tgt_rows, f32), ((tgt_size, src_size), f32), (tgt_rows, f32), (src_rows, f32), row_out],
        [tgt_spread, row_ratio, row_part],
        "row_pass_2",
    )
    def product(got, terms, weight, rows, out, spread_rows, part, last):
        args, kept = [got, terms, weight], (rows, f32)
        if not last:
            kernel = functools.partial(product_kernel, float(total))
            return None, call(kernel, args, [out], [spread_rows, part, pltpu.VMEM(*kept)], "product")[0]
        kernel = functools.partial(last_product_kernel, float(total))
        return call(kernel, args, [kept, out], [spread_rows, part], "last_product")

    for step in range(2, ITERS + 1):
        last = step == ITERS
        got = exchange(sent, SRC_GROUP)
        f_factor, sent = product(got, terms, weight, src_rows, col_out, src_spread, col_part, last)
        got = exchange(sent, TGT_GROUP)
        g_factor, sent = product(got, mate, one, tgt_rows, row_out, tgt_spread, row_part, last)
    got = exchange(sent, SRC_GROUP)
    sent, own_src, own_tgt = call(
        functools.partial(last_kernel, shift),
        [got, f, g, f_factor, g_factor],
        [((tgt_count, 1, LANES), f32), ((1, per_dev), f32), ((1, per_dev), f32)],
        [],
        "mismatch",
    )
    squares = jnp.sum(exchange(sent, TGT_GROUP)[:, 0, 0])
    return own_src[0], own_tgt[0], jnp.sqrt(squares / total)


def solution(mesh, shape=(4, 4, 2, 4, 2)):
    placed = Mesh(mesh.devices.reshape(shape), AXES)
    return jax.shard_map(
        on_device,
        mesh=placed,
        in_specs=(P(None, AXES), P(None, AXES), P(AXES), P(AXES)),
        out_specs=(P(AXES), P(AXES), P()),
        check_vma=False,
    )
```

```python
import functools
import math

import jax
import jax.numpy as jnp
from jax import lax
from jax.experimental import pallas as pl
from jax.experimental.pallas import tpu as pltpu
from jax.sharding import Mesh, PartitionSpec as P

EPS = 0.02
ITERS = 3
LANES = 128
TAIL = 16
PACK = 16
BLOCKS = 2
WIDTH = BLOCKS * LANES
GROUPS = 64
VMEM = 8 * 1024 * 1024
UNIT = 1.0 / (EPS * math.log(2.0))
AXES = ("x", "zh", "zl", "y", "c")
SRC_GROUP = ("x", "y")
TGT_GROUP = ("zh", "zl", "c")

f32 = jnp.float32
bf16 = jnp.bfloat16


def log2(value):
    return jnp.log(value) * (1.0 / math.log(2.0))


def pieces(value):
    high = value.astype(bf16).astype(f32)
    rest = value - high
    middle = rest.astype(bf16).astype(f32)
    low = (rest - middle).astype(bf16).astype(f32)
    return high, middle, low


def stack(rows, width):
    index = lax.broadcasted_iota(jnp.int32, (TAIL, width), 0)
    out = jnp.zeros((TAIL, width), f32)
    for place, row in rows:
        out = jnp.where(index == place, row, out)
    return out


def prepare(blocks, wide_ref, tail_ref, raw_ref, scale_ref):
    depth = raw_ref.shape[0]
    for cells, place in blocks:
        at = pl.ds(pl.multiple_of(place * LANES, LANES), LANES)
        embed = cells[:depth, :]
        raw_ref[:, at] = embed
        value = embed.astype(f32)
        weight = cells[depth : depth + PACK, :].astype(f32)[0:1]
        norm = jnp.sum(value * value, axis=0, keepdims=True)
        scale_ref[pl.ds(place, 1), :] = weight * (UNIT / depth)
        scaled = (2.0 * weight) * value
        high = scaled.astype(bf16).astype(f32)
        low = scaled - high
        one = jnp.ones_like(weight)
        n = pieces(norm)
        wn = pieces(weight * norm)
        tail_ref[:, at] = stack([(0, one), (1, one), (2, one), (3, n[0]), (4, n[1]), (5, n[2])], LANES)
        tail = stack(
            [(0, -wn[0]), (1, -wn[1]), (2, -wn[2])]
            + [(3, -weight), (4, -weight), (5, -weight), (6, one), (7, one), (8, one)],
            LANES,
        )
        wide_ref[at, :] = jnp.concatenate([high, low, tail], axis=0).T.astype(bf16)


def spread(summed, rows_ref):
    column = summed.T
    for b in range(rows_ref.shape[0] // LANES):
        rows_ref[pl.ds(b * LANES, LANES), :] = jnp.broadcast_to(column[:, b : b + 1], (LANES, LANES))


def strip_of(s):
    return pl.ds(s * WIDTH, WIDTH) if isinstance(s, int) else pl.ds(pl.multiple_of(s * WIDTH, WIDTH), WIDTH)


def get(ref, s):
    return jnp.concatenate([ref[pl.ds(BLOCKS * s + k, 1), :] for k in range(BLOCKS)], axis=1)


def put(ref, s, value):
    for k in range(BLOCKS):
        ref[pl.ds(BLOCKS * s + k, 1), :] = value[:, k * LANES : (k + 1) * LANES]


def strip_score(s, count, operands, rows_ref, ratio_ref):
    wide_ref, raw_ref, tail_ref, scale_ref = operands
    at = strip_of(s)
    tail = tail_ref[:, at]
    if ratio_ref is not None:
        tail = tail + stack([(6 + k, get(ratio_ref.at[k], s)) for k in range(3)], WIDTH)
    raw = raw_ref[:, at]
    operand = jnp.concatenate([raw, raw, tail.astype(bf16)], axis=0)
    score = jnp.dot(wide_ref[:count, :], operand, preferred_element_type=f32) * get(scale_ref, s)
    if rows_ref is not None:
        rows = rows_ref[:count, :]
        score = score + jnp.concatenate([rows] * BLOCKS, axis=1)
    return score


def strips(count, body, unroll):
    if unroll:
        for s in range(count):
            body(s)
    else:

        def step(s, carry):
            body(s)
            return carry

        lax.fori_loop(0, count, step, 0)


def find_tops(count, operands, rows_ref, top_ref, unroll=True):
    def body(s):
        put(top_ref, s, jnp.max(strip_score(s, count, operands, rows_ref, None), axis=0, keepdims=True))

    strips(top_ref.shape[0] // BLOCKS, body, unroll)


def sum_pass(operands, rows_ref, kept, ratio_ref, part_ref, terms_ref=None, unroll=True):
    for k, piece in enumerate(pieces(kept / operands[3][...])):
        ratio_ref[k] = piece

    def body(s):
        terms = jnp.exp2(strip_score(s, operands[0].shape[0], operands, rows_ref, ratio_ref))
        if terms_ref is not None:
            terms_ref[:, strip_of(s)] = terms
        put(part_ref, s, jnp.sum(terms, axis=0, keepdims=True))

    strips(part_ref.shape[0] // BLOCKS, body, unroll)


def log_pass(operands, rows_ref, ratio_ref, part_ref, top_ref, head, margin, large, terms_ref=None):
    size = operands[0].shape[0]
    find_tops(min(head, size), operands, rows_ref, top_ref)
    top_ref[...] = top_ref[...] + margin
    sum_pass(operands, rows_ref, -top_ref[...], ratio_ref, part_ref, terms_ref)

    @pl.when(jnp.logical_not(jnp.max(part_ref[...]) < large))
    def _():
        find_tops(size, operands, rows_ref, top_ref, unroll=False)
        sum_pass(operands, rows_ref, -top_ref[...], ratio_ref, part_ref, terms_ref, unroll=False)


def product_pass(terms_ref, factor, rows_ref, part_ref):
    spread(factor, rows_ref)
    size = terms_ref.shape[1]

    def step(g, total):
        for q in range(GROUPS):
            at = pl.ds(pl.multiple_of((g * GROUPS + q) * 8, 8), 8)
            total = total + terms_ref[at, :] * jnp.concatenate([rows_ref[at, :]] * (size // LANES), axis=1)
        return total

    total = lax.fori_loop(0, terms_ref.shape[0] // (8 * GROUPS), step, jnp.zeros((8, size), f32))
    total = jnp.sum(total, axis=0, keepdims=True)
    for b in range(size // LANES):
        part_ref[b : b + 1, :] = total[:, b * LANES : (b + 1) * LANES]


def combine_logs(got_ref, shift):
    got = got_ref[...]
    top = jnp.max(got, axis=0)
    return -(top + log2(jnp.sum(jnp.exp2(got - top[None]), axis=0))) - shift


def combine_sums(got_ref, total):
    return 1.0 / (total * jnp.sum(got_ref[...], axis=0))


def send(part, out_ref):
    out_ref[...] = jnp.broadcast_to(part[None], out_ref.shape)


def pack_kernel(src_embed, tgt_embed, src_weight, tgt_weight, src_out, tgt_out, embeds, weights, sems):
    copies = [
        pltpu.make_async_copy(source, target, sems.at[k])
        for k, (source, target) in enumerate(
            [
                (src_embed, embeds.at[0]),
                (tgt_embed, embeds.at[1]),
                (src_weight, weights.at[0]),
                (tgt_weight, weights.at[1]),
            ]
        )
    ]
    for copy in copies:
        copy.start()
    for copy in copies:
        copy.wait()
    for k, out in enumerate((src_out, tgt_out)):
        row = jnp.broadcast_to(weights[k].astype(f32), (PACK, LANES)).astype(bf16)
        send(jnp.concatenate([embeds[k], row], axis=0), out)


def sources_kernel(own, far, _, wide, tail, raw, scale):
    x, y = lax.axis_index("x"), lax.axis_index("y")
    blocks = []
    for m in range(4):
        for k in range(4):
            ref = (own.at[k] if m == 0 else far.at[m - 1, k])
            blocks.append((ref, (x ^ k) * 4 + (y ^ m)))
    prepare(blocks, wide, tail, raw, scale)


def targets_kernel(own, other, wide, tail, raw, scale):
    core = lax.axis_index("c")
    blocks = [(own.at[z], 2 * z + core) for z in range(own.shape[0])]
    blocks += [(other.at[z], 2 * z + 1 - core) for z in range(own.shape[0])]
    prepare(blocks, wide, tail, raw, scale)


def first_kernel(wide, raw, tail, scale, out, ratio, part, top):
    log_pass((wide, raw, tail, scale), None, ratio, part, top, 512, 100.0, 2.0**120)
    send(top[...] + log2(part[...]), out)


def second_kernel(shift, got, wide, raw, tail, scale, new, part, lse, terms, out, rows, ratio, top):
    new[...] = combine_logs(got, shift)
    spread(new[...], rows)
    log_pass((wide, raw, tail, scale), rows, ratio, part, top, 128, 30.0, 2.0**80, terms)
    lse[...] = top[...] + log2(part[...])
    send(lse[...], out)


def third_kernel(shift, got, kept, lse, mass, wide, raw, tail, scale, new, terms, weight, one, out, rows, ratio, part):
    new[...] = combine_logs(got, shift)
    weight[...] = jnp.exp2(lse[...] + new[...]) / mass[...]
    one[...] = jnp.ones_like(one)
    spread(new[...], rows)
    sum_pass((wide, raw, tail, scale), rows, kept[...], ratio, part, terms)
    send(part[...], out)


def product_kernel(total, got, terms, weight, out, rows, part, factor):
    factor[...] = combine_sums(got, total)
    product_pass(terms, factor[...], rows, part)
    send(part[...] * weight[...], out)


def last_product_kernel(total, got, terms, weight, factor, out, rows, part):
    product_kernel(total, got, terms, weight, out, rows, part, factor)


def last_kernel(total, got, f, g, f_factor, g_factor, out, own_src, own_tgt):
    diff = jnp.log(f_factor[...] * (total * jnp.sum(got[...], axis=0)))
    out[...] = jnp.full(out.shape, jnp.sum(diff * diff), f32)
    at = pl.ds(lax.axis_index(SRC_GROUP), 1)
    own_src[...] = (f[at, :] + log2(f_factor[at, :])) * (1.0 / UNIT)
    at = pl.ds(lax.axis_index(TGT_GROUP), 1)
    own_tgt[...] = (g[at, :] + log2(g_factor[at, :])) * (1.0 / UNIT)


def call(kernel, args, outs, scratch, name):
    return pl.pallas_call(
        kernel,
        out_shape=[jax.ShapeDtypeStruct(shape, dtype) for shape, dtype in outs],
        in_specs=[pl.BlockSpec(memory_space=pltpu.VMEM)] * len(args),
        out_specs=[pl.BlockSpec(memory_space=pltpu.VMEM)] * len(outs),
        scratch_shapes=scratch,
        compiler_params=pltpu.CompilerParams(vmem_limit_bytes=VMEM),
        name=name,
    )(*args)


def exchange(sent, group):
    return lax.all_to_all(sent, group, 0, 0)


def on_device(src_embed, tgt_embed, src_weight, tgt_weight):
    depth, per_dev = src_embed.shape
    src_count, tgt_count = lax.axis_size(SRC_GROUP), lax.axis_size(TGT_GROUP)
    total = per_dev * src_count * tgt_count
    shift = math.log2(total)
    src_size, tgt_size = per_dev * src_count, per_dev * tgt_count
    src_rows, tgt_rows = (src_count, per_dev), (tgt_count, per_dev)

    cells = (depth + PACK, per_dev)
    z_count = tgt_count // lax.axis_size("c")
    src_sent, tgt_sent = pl.pallas_call(
        pack_kernel,
        out_shape=[
            pltpu.VMEM((1,) + cells, bf16),
            pltpu.VMEM((z_count,) + cells, bf16),
        ],
        in_specs=[pl.BlockSpec(memory_space=pl.ANY)] * 4,
        out_specs=[pl.BlockSpec(memory_space=pltpu.VMEM)] * 2,
        scratch_shapes=[
            pltpu.VMEM((2, depth, per_dev), bf16),
            pltpu.VMEM((2, 1, per_dev), bf16),
            pltpu.SemaphoreType.DMA((4,)),
        ],
        name="pack",
    )(src_embed, tgt_embed, src_weight[None], tgt_weight[None])

    def neighbours(array, axis):
        size = lax.axis_size(axis)
        return [lax.ppermute(array, axis, [(i, i ^ k) for i in range(size)]) for k in range(1, size)]

    tgt = exchange(tgt_sent, ("zh", "zl"))
    src = jnp.concatenate([src_sent] + neighbours(src_sent, "x"), axis=0)
    src_far = jnp.stack(neighbours(src, "y"))
    (tgt_other,) = neighbours(tgt, "c")

    wide = 2 * depth + TAIL

    def operands(size, rows):
        return [((size, wide), bf16), ((TAIL, size), f32), ((depth, size), bf16), (rows, f32)]

    row_out = ((src_count,) + src_rows, f32)
    col_out = ((tgt_count,) + tgt_rows, f32)
    row_part = pltpu.VMEM(src_rows, f32)
    col_part = pltpu.VMEM(tgt_rows, f32)
    row_ratio = pltpu.VMEM((3,) + src_rows, f32)
    col_ratio = pltpu.VMEM((3,) + tgt_rows, f32)

    t_wide, t_tail, t_raw, t_scale = call(
        targets_kernel, [tgt, tgt_other], operands(tgt_size, tgt_rows), [], "targets"
    )
    s_wide, s_tail, s_raw, s_scale = call(
        sources_kernel, [src, src_far, t_scale], operands(src_size, src_rows), [], "sources"
    )
    (sent,) = call(
        first_kernel,
        [t_wide, s_raw, s_tail, s_scale],
        [row_out],
        [row_ratio, row_part, row_part],
        "row_pass_1",
    )
    got = exchange(sent, SRC_GROUP)
    src_spread = pltpu.VMEM((src_size, LANES), f32)
    tgt_spread = pltpu.VMEM((tgt_size, LANES), f32)
    keep_tgt = [t_raw, t_tail, t_scale]
    keep_src = [s_raw, s_tail, s_scale]

    f, part, lse, terms, sent = call(
        functools.partial(second_kernel, shift),
        [got, s_wide] + keep_tgt,
        [(src_rows, f32), (tgt_rows, f32), (tgt_rows, f32), ((src_size, tgt_size), f32), col_out],
        [src_spread, col_ratio, col_part],
        "col_pass_1",
    )
    got = exchange(sent, TGT_GROUP)
    g, mate, weight, one, sent = call(
        functools.partial(third_kernel, shift),
        [got, f, lse, part, t_wide] + keep_src,
        [(tgt_rows, f32), ((tgt_size, src_size), f32), (tgt_rows, f32), (src_rows, f32), row_out],
        [tgt_spread, row_ratio, row_part],
        "row_pass_2",
    )
    def product(got, terms, weight, rows, out, spread_rows, part, last):
        args, kept = [got, terms, weight], (rows, f32)
        if not last:
            kernel = functools.partial(product_kernel, float(total))
            return None, call(kernel, args, [out], [spread_rows, part, pltpu.VMEM(*kept)], "product")[0]
        kernel = functools.partial(last_product_kernel, float(total))
        return call(kernel, args, [kept, out], [spread_rows, part], "last_product")

    for step in range(2, ITERS + 1):
        last = step == ITERS
        got = exchange(sent, SRC_GROUP)
        f_factor, sent = product(got, terms, weight, src_rows, col_out, src_spread, col_part, last)
        got = exchange(sent, TGT_GROUP)
        g_factor, sent = product(got, mate, one, tgt_rows, row_out, tgt_spread, row_part, last)
    got = exchange(sent, SRC_GROUP)
    sent, own_src, own_tgt = call(
        functools.partial(last_kernel, float(total)),
        [got, f, g, f_factor, g_factor],
        [((tgt_count, 1, LANES), f32), ((1, per_dev), f32), ((1, per_dev), f32)],
        [],
        "mismatch",
    )
    squares = jnp.sum(exchange(sent, TGT_GROUP)[:, 0, 0])
    return own_src[0], own_tgt[0], jnp.sqrt(squares / total)


def solution(mesh, shape=(4, 4, 2, 4, 2)):
    placed = Mesh(mesh.devices.reshape(shape), AXES)
    return jax.shard_map(
        on_device,
        mesh=placed,
        in_specs=(P(None, AXES), P(None, AXES), P(AXES), P(AXES)),
        out_specs=(P(AXES), P(AXES), P()),
        check_vma=False,
    )
```

```python
import functools
import math

import jax
import jax.numpy as jnp
from jax import lax
from jax.experimental import pallas as pl
from jax.experimental.pallas import tpu as pltpu
from jax.sharding import Mesh, PartitionSpec as P

EPS = 0.02
ITERS = 3
LANES = 128
TAIL = 16
PACK = 16
BLOCKS = 2
WIDTH = BLOCKS * LANES
GROUPS = 64
VMEM = 8 * 1024 * 1024
UNIT = 1.0 / (EPS * math.log(2.0))
AXES = ("x", "zh", "zl", "y", "c")
SRC_GROUP = ("x", "y")
TGT_GROUP = ("zh", "zl", "c")

f32 = jnp.float32
bf16 = jnp.bfloat16


def log2(value):
    return jnp.log(value) * (1.0 / math.log(2.0))


def pieces(value):
    high = value.astype(bf16).astype(f32)
    rest = value - high
    middle = rest.astype(bf16).astype(f32)
    low = (rest - middle).astype(bf16).astype(f32)
    return high, middle, low


def stack(rows, width):
    index = lax.broadcasted_iota(jnp.int32, (TAIL, width), 0)
    out = jnp.zeros((TAIL, width), f32)
    for place, row in rows:
        out = jnp.where(index == place, row, out)
    return out


def prepare(blocks, wide_ref, tail_ref, raw_ref, scale_ref):
    depth = raw_ref.shape[0]
    for cells, place in blocks:
        at = pl.ds(pl.multiple_of(place * LANES, LANES), LANES)
        embed = cells[:depth, :]
        raw_ref[:, at] = embed
        value = embed.astype(f32)
        weight = cells[depth : depth + PACK, :].astype(f32)[0:1]
        norm = jnp.sum(value * value, axis=0, keepdims=True)
        scale_ref[pl.ds(place, 1), :] = weight * (UNIT / depth)
        scaled = (2.0 * weight) * value
        high = scaled.astype(bf16).astype(f32)
        low = scaled - high
        one = jnp.ones_like(weight)
        n = pieces(norm)
        wn = pieces(weight * norm)
        tail_ref[:, at] = stack([(0, one), (1, one), (2, one), (3, n[0]), (4, n[1]), (5, n[2])], LANES)
        tail = stack(
            [(0, -wn[0]), (1, -wn[1]), (2, -wn[2])]
            + [(3, -weight), (4, -weight), (5, -weight), (6, one), (7, one), (8, one)],
            LANES,
        )
        wide_ref[at, :] = jnp.concatenate([high, low, tail], axis=0).T.astype(bf16)


def spread(summed, rows_ref):
    column = summed.T
    for b in range(rows_ref.shape[0] // LANES):
        rows_ref[pl.ds(b * LANES, LANES), :] = jnp.broadcast_to(column[:, b : b + 1], (LANES, LANES))


def strip_of(s):
    return pl.ds(s * WIDTH, WIDTH) if isinstance(s, int) else pl.ds(pl.multiple_of(s * WIDTH, WIDTH), WIDTH)


def get(ref, s):
    return jnp.concatenate([ref[pl.ds(BLOCKS * s + k, 1), :] for k in range(BLOCKS)], axis=1)


def put(ref, s, value):
    for k in range(BLOCKS):
        ref[pl.ds(BLOCKS * s + k, 1), :] = value[:, k * LANES : (k + 1) * LANES]


def strip_score(s, count, operands, rows_ref, ratio_ref):
    wide_ref, raw_ref, tail_ref, scale_ref = operands
    at = strip_of(s)
    tail = tail_ref[:, at]
    if ratio_ref is not None:
        tail = tail + stack([(6 + k, get(ratio_ref.at[k], s)) for k in range(3)], WIDTH)
    raw = raw_ref[:, at]
    operand = jnp.concatenate([raw, raw, tail.astype(bf16)], axis=0)
    score = jnp.dot(wide_ref[:count, :], operand, preferred_element_type=f32) * get(scale_ref, s)
    if rows_ref is not None:
        rows = rows_ref[:count, :]
        score = score + jnp.concatenate([rows] * BLOCKS, axis=1)
    return score


def strips(count, body, unroll):
    if unroll:
        for s in range(count):
            body(s)
    else:

        def step(s, carry):
            body(s)
            return carry

        lax.fori_loop(0, count, step, 0)


def find_tops(count, operands, rows_ref, top_ref, unroll=True):
    def body(s):
        put(top_ref, s, jnp.max(strip_score(s, count, operands, rows_ref, None), axis=0, keepdims=True))

    strips(top_ref.shape[0] // BLOCKS, body, unroll)


def sum_pass(operands, rows_ref, kept, ratio_ref, part_ref, terms_ref=None, unroll=True):
    for k, piece in enumerate(pieces(kept / operands[3][...])):
        ratio_ref[k] = piece

    def body(s):
        terms = jnp.exp2(strip_score(s, operands[0].shape[0], operands, rows_ref, ratio_ref))
        if terms_ref is not None:
            terms_ref[:, strip_of(s)] = terms
        put(part_ref, s, jnp.sum(terms, axis=0, keepdims=True))

    strips(part_ref.shape[0] // BLOCKS, body, unroll)


def log_pass(operands, rows_ref, ratio_ref, part_ref, top_ref, head, margin, large, terms_ref=None):
    size = operands[0].shape[0]
    find_tops(min(head, size), operands, rows_ref, top_ref)
    top_ref[...] = top_ref[...] + margin
    sum_pass(operands, rows_ref, -top_ref[...], ratio_ref, part_ref, terms_ref)

    @pl.when(jnp.logical_not(jnp.max(part_ref[...]) < large))
    def _():
        find_tops(size, operands, rows_ref, top_ref, unroll=False)
        sum_pass(operands, rows_ref, -top_ref[...], ratio_ref, part_ref, terms_ref, unroll=False)


def product_pass(terms_ref, factor, rows_ref, part_ref):
    spread(factor, rows_ref)
    size = terms_ref.shape[1]

    def step(g, total):
        for q in range(GROUPS):
            at = pl.ds(pl.multiple_of((g * GROUPS + q) * 8, 8), 8)
            total = total + terms_ref[at, :] * jnp.concatenate([rows_ref[at, :]] * (size // LANES), axis=1)
        return total

    total = lax.fori_loop(0, terms_ref.shape[0] // (8 * GROUPS), step, jnp.zeros((8, size), f32))
    total = jnp.sum(total, axis=0, keepdims=True)
    for b in range(size // LANES):
        part_ref[b : b + 1, :] = total[:, b * LANES : (b + 1) * LANES]


def combine_logs(got_ref, shift):
    got = got_ref[...]
    top = jnp.max(got, axis=0)
    return -(top + log2(jnp.sum(jnp.exp2(got - top[None]), axis=0))) - shift


def combine_sums(got_ref, total):
    return 1.0 / (total * jnp.sum(got_ref[...], axis=0))


def send(part, out_ref):
    out_ref[...] = jnp.broadcast_to(part[None], out_ref.shape)


def pack_kernel(src_embed, tgt_embed, src_weight, tgt_weight, src_out, tgt_out, embeds, weights, sems):
    copies = [
        pltpu.make_async_copy(source, target, sems.at[k])
        for k, (source, target) in enumerate(
            [
                (src_embed, embeds.at[0]),
                (tgt_embed, embeds.at[1]),
                (src_weight, weights.at[0]),
                (tgt_weight, weights.at[1]),
            ]
        )
    ]
    for copy in copies:
        copy.start()
    for copy in copies:
        copy.wait()
    for k, out in enumerate((src_out, tgt_out)):
        row = jnp.broadcast_to(weights[k].astype(f32), (PACK, LANES)).astype(bf16)
        send(jnp.concatenate([embeds[k], row], axis=0), out)


def first_kernel(
    src_own, src_far, tgt_own, tgt_other, s_wide, s_tail, s_raw, s_scale, t_wide, t_tail, t_raw, t_scale, out, ratio, part, top
):
    x, y, core = lax.axis_index("x"), lax.axis_index("y"), lax.axis_index("c")
    blocks = [(tgt_own.at[z], 2 * z + core) for z in range(tgt_own.shape[0])]
    blocks += [(tgt_other.at[z], 2 * z + 1 - core) for z in range(tgt_own.shape[0])]
    prepare(blocks, t_wide, t_tail, t_raw, t_scale)
    blocks = []
    for m in range(4):
        for k in range(4):
            ref = src_own.at[k] if m == 0 else src_far.at[m - 1, k]
            blocks.append((ref, (x ^ k) * 4 + (y ^ m)))
    prepare(blocks, s_wide, s_tail, s_raw, s_scale)
    log_pass((t_wide, s_raw, s_tail, s_scale), None, ratio, part, top, 512, 100.0, 2.0**120)
    send(top[...] + log2(part[...]), out)


def second_kernel(shift, got, wide, raw, tail, scale, new, part, lse, terms, out, rows, ratio, top):
    new[...] = combine_logs(got, shift)
    spread(new[...], rows)
    log_pass((wide, raw, tail, scale), rows, ratio, part, top, 128, 30.0, 2.0**80, terms)
    lse[...] = top[...] + log2(part[...])
    send(lse[...], out)


def third_kernel(shift, got, kept, lse, mass, wide, raw, tail, scale, new, terms, weight, one, out, rows, ratio, part):
    new[...] = combine_logs(got, shift)
    weight[...] = jnp.exp2(lse[...] + new[...]) / mass[...]
    one[...] = jnp.ones_like(one)
    spread(new[...], rows)
    sum_pass((wide, raw, tail, scale), rows, kept[...], ratio, part, terms)
    send(part[...], out)


def product_kernel(total, got, terms, weight, out, rows, part, factor):
    factor[...] = combine_sums(got, total)
    product_pass(terms, factor[...], rows, part)
    send(part[...] * weight[...], out)


def last_product_kernel(total, got, terms, weight, factor, out, rows, part):
    product_kernel(total, got, terms, weight, out, rows, part, factor)


def last_kernel(total, got, f, g, f_factor, g_factor, out, own_src, own_tgt):
    diff = jnp.log(f_factor[...] * (total * jnp.sum(got[...], axis=0)))
    out[...] = jnp.full(out.shape, jnp.sum(diff * diff), f32)
    at = pl.ds(lax.axis_index(SRC_GROUP), 1)
    own_src[...] = (f[at, :] + log2(f_factor[at, :])) * (1.0 / UNIT)
    at = pl.ds(lax.axis_index(TGT_GROUP), 1)
    own_tgt[...] = (g[at, :] + log2(g_factor[at, :])) * (1.0 / UNIT)


def call(kernel, args, outs, scratch, name):
    return pl.pallas_call(
        kernel,
        out_shape=[jax.ShapeDtypeStruct(shape, dtype) for shape, dtype in outs],
        in_specs=[pl.BlockSpec(memory_space=pltpu.VMEM)] * len(args),
        out_specs=[pl.BlockSpec(memory_space=pltpu.VMEM)] * len(outs),
        scratch_shapes=scratch,
        compiler_params=pltpu.CompilerParams(vmem_limit_bytes=VMEM),
        name=name,
    )(*args)


def exchange(sent, group):
    return lax.all_to_all(sent, group, 0, 0)


def on_device(src_embed, tgt_embed, src_weight, tgt_weight):
    depth, per_dev = src_embed.shape
    src_count, tgt_count = lax.axis_size(SRC_GROUP), lax.axis_size(TGT_GROUP)
    total = per_dev * src_count * tgt_count
    shift = math.log2(total)
    src_size, tgt_size = per_dev * src_count, per_dev * tgt_count
    src_rows, tgt_rows = (src_count, per_dev), (tgt_count, per_dev)

    cells = (depth + PACK, per_dev)
    z_count = tgt_count // lax.axis_size("c")
    src_sent, tgt_sent = pl.pallas_call(
        pack_kernel,
        out_shape=[
            pltpu.VMEM((1,) + cells, bf16),
            pltpu.VMEM((z_count,) + cells, bf16),
        ],
        in_specs=[pl.BlockSpec(memory_space=pl.ANY)] * 4,
        out_specs=[pl.BlockSpec(memory_space=pltpu.VMEM)] * 2,
        scratch_shapes=[
            pltpu.VMEM((2, depth, per_dev), bf16),
            pltpu.VMEM((2, 1, per_dev), bf16),
            pltpu.SemaphoreType.DMA((4,)),
        ],
        name="pack",
    )(src_embed, tgt_embed, src_weight[None], tgt_weight[None])

    def neighbours(array, axis):
        size = lax.axis_size(axis)
        return [lax.ppermute(array, axis, [(i, i ^ k) for i in range(size)]) for k in range(1, size)]

    tgt = exchange(tgt_sent, ("zh", "zl"))
    src = jnp.concatenate([src_sent] + neighbours(src_sent, "x"), axis=0)
    src_far = jnp.stack(neighbours(src, "y"))
    (tgt_other,) = neighbours(tgt, "c")

    wide = 2 * depth + TAIL

    def operands(size, rows):
        return [((size, wide), bf16), ((TAIL, size), f32), ((depth, size), bf16), (rows, f32)]

    row_out = ((src_count,) + src_rows, f32)
    col_out = ((tgt_count,) + tgt_rows, f32)
    row_part = pltpu.VMEM(src_rows, f32)
    col_part = pltpu.VMEM(tgt_rows, f32)
    row_ratio = pltpu.VMEM((3,) + src_rows, f32)
    col_ratio = pltpu.VMEM((3,) + tgt_rows, f32)

    s_wide, s_tail, s_raw, s_scale, t_wide, t_tail, t_raw, t_scale, sent = call(
        first_kernel,
        [src, src_far, tgt, tgt_other],
        operands(src_size, src_rows) + operands(tgt_size, tgt_rows) + [row_out],
        [row_ratio, row_part, row_part],
        "row_pass_1",
    )
    got = exchange(sent, SRC_GROUP)
    src_spread = pltpu.VMEM((src_size, LANES), f32)
    tgt_spread = pltpu.VMEM((tgt_size, LANES), f32)
    keep_tgt = [t_raw, t_tail, t_scale]
    keep_src = [s_raw, s_tail, s_scale]

    f, part, lse, terms, sent = call(
        functools.partial(second_kernel, shift),
        [got, s_wide] + keep_tgt,
        [(src_rows, f32), (tgt_rows, f32), (tgt_rows, f32), ((src_size, tgt_size), f32), col_out],
        [src_spread, col_ratio, col_part],
        "col_pass_1",
    )
    got = exchange(sent, TGT_GROUP)
    g, mate, weight, one, sent = call(
        functools.partial(third_kernel, shift),
        [got, f, lse, part, t_wide] + keep_src,
        [(tgt_rows, f32), ((tgt_size, src_size), f32), (tgt_rows, f32), (src_rows, f32), row_out],
        [tgt_spread, row_ratio, row_part],
        "row_pass_2",
    )
    def product(got, terms, weight, rows, out, spread_rows, part, last):
        args, kept = [got, terms, weight], (rows, f32)
        if not last:
            kernel = functools.partial(product_kernel, float(total))
            return None, call(kernel, args, [out], [spread_rows, part, pltpu.VMEM(*kept)], "product")[0]
        kernel = functools.partial(last_product_kernel, float(total))
        return call(kernel, args, [kept, out], [spread_rows, part], "last_product")

    for step in range(2, ITERS + 1):
        last = step == ITERS
        got = exchange(sent, SRC_GROUP)
        f_factor, sent = product(got, terms, weight, src_rows, col_out, src_spread, col_part, last)
        got = exchange(sent, TGT_GROUP)
        g_factor, sent = product(got, mate, one, tgt_rows, row_out, tgt_spread, row_part, last)
    got = exchange(sent, SRC_GROUP)
    sent, own_src, own_tgt = call(
        functools.partial(last_kernel, float(total)),
        [got, f, g, f_factor, g_factor],
        [((tgt_count, 1, LANES), f32), ((1, per_dev), f32), ((1, per_dev), f32)],
        [],
        "mismatch",
    )
    squares = jnp.sum(exchange(sent, TGT_GROUP)[:, 0, 0])
    return own_src[0], own_tgt[0], jnp.sqrt(squares / total)


def solution(mesh, shape=(4, 4, 2, 4, 2)):
    placed = Mesh(mesh.devices.reshape(shape), AXES)
    return jax.shard_map(
        on_device,
        mesh=placed,
        in_specs=(P(None, AXES), P(None, AXES), P(AXES), P(AXES)),
        out_specs=(P(AXES), P(AXES), P()),
        check_vma=False,
    )
```

```python
import functools
import math

import jax
import jax.numpy as jnp
from jax import lax
from jax.experimental import pallas as pl
from jax.experimental.pallas import tpu as pltpu
from jax.sharding import Mesh, PartitionSpec as P

EPS = 0.02
ITERS = 3
LANES = 128
TAIL = 16
PACK = 16
BLOCKS = 2
WIDTH = BLOCKS * LANES
GROUPS = 64
VMEM = 8 * 1024 * 1024
UNIT = 1.0 / (EPS * math.log(2.0))
AXES = ("x", "zh", "zl", "y", "c")
SRC_GROUP = ("x", "y")
TGT_GROUP = ("zh", "zl", "c")

f32 = jnp.float32
bf16 = jnp.bfloat16


def log2(value):
    return jnp.log(value) * (1.0 / math.log(2.0))


def pieces(value):
    high = value.astype(bf16).astype(f32)
    rest = value - high
    middle = rest.astype(bf16).astype(f32)
    low = (rest - middle).astype(bf16).astype(f32)
    return high, middle, low


def stack(rows, width):
    index = lax.broadcasted_iota(jnp.int32, (TAIL, width), 0)
    out = jnp.zeros((TAIL, width), f32)
    for place, row in rows:
        out = jnp.where(index == place, row, out)
    return out


def prepare(blocks, wide_ref, tail_ref, raw_ref, scale_ref):
    depth = raw_ref.shape[0]
    for cells, place in blocks:
        at = pl.ds(pl.multiple_of(place * LANES, LANES), LANES)
        embed = cells[:depth, :]
        raw_ref[:, at] = embed
        value = embed.astype(f32)
        weight = cells[depth : depth + PACK, :].astype(f32)[0:1]
        norm = jnp.sum(value * value, axis=0, keepdims=True)
        scale_ref[pl.ds(place, 1), :] = weight * (UNIT / depth)
        scaled = (2.0 * weight) * value
        high = scaled.astype(bf16).astype(f32)
        low = scaled - high
        one = jnp.ones_like(weight)
        n = pieces(norm)
        wn = pieces(weight * norm)
        tail_ref[:, at] = stack([(0, one), (1, one), (2, one), (3, n[0]), (4, n[1]), (5, n[2])], LANES)
        tail = stack(
            [(0, -wn[0]), (1, -wn[1]), (2, -wn[2])]
            + [(3, -weight), (4, -weight), (5, -weight), (6, one), (7, one), (8, one)],
            LANES,
        )
        wide_ref[at, :] = jnp.concatenate([high, low, tail], axis=0).T.astype(bf16)


def spread(summed, rows_ref):
    column = summed.T
    for b in range(rows_ref.shape[0] // LANES):
        rows_ref[pl.ds(b * LANES, LANES), :] = jnp.broadcast_to(column[:, b : b + 1], (LANES, LANES))


def strip_of(s):
    return pl.ds(s * WIDTH, WIDTH) if isinstance(s, int) else pl.ds(pl.multiple_of(s * WIDTH, WIDTH), WIDTH)


def get(ref, s):
    return jnp.concatenate([ref[pl.ds(BLOCKS * s + k, 1), :] for k in range(BLOCKS)], axis=1)


def put(ref, s, value):
    for k in range(BLOCKS):
        ref[pl.ds(BLOCKS * s + k, 1), :] = value[:, k * LANES : (k + 1) * LANES]


def strip_score(s, count, operands, rows_ref, ratio_ref):
    wide_ref, raw_ref, tail_ref, scale_ref = operands
    at = strip_of(s)
    tail = tail_ref[:, at]
    if ratio_ref is not None:
        tail = tail + stack([(6 + k, get(ratio_ref.at[k], s)) for k in range(3)], WIDTH)
    raw = raw_ref[:, at]
    operand = jnp.concatenate([raw, raw, tail.astype(bf16)], axis=0)
    score = jnp.dot(wide_ref[:count, :], operand, preferred_element_type=f32) * get(scale_ref, s)
    if rows_ref is not None:
        rows = rows_ref[:count, :]
        score = score + jnp.concatenate([rows] * BLOCKS, axis=1)
    return score


def strips(count, body, unroll):
    if unroll:
        for s in range(count):
            body(s)
    else:

        def step(s, carry):
            body(s)
            return carry

        lax.fori_loop(0, count, step, 0)


def find_tops(count, operands, rows_ref, top_ref, unroll=True):
    def body(s):
        put(top_ref, s, jnp.max(strip_score(s, count, operands, rows_ref, None), axis=0, keepdims=True))

    strips(top_ref.shape[0] // BLOCKS, body, unroll)


def sum_pass(operands, rows_ref, kept, ratio_ref, part_ref, terms_ref=None, unroll=True):
    for k, piece in enumerate(pieces(kept / operands[3][...])):
        ratio_ref[k] = piece

    def body(s):
        terms = jnp.exp2(strip_score(s, operands[0].shape[0], operands, rows_ref, ratio_ref))
        if terms_ref is not None:
            terms_ref[:, strip_of(s)] = terms
        put(part_ref, s, jnp.sum(terms, axis=0, keepdims=True))

    strips(part_ref.shape[0] // BLOCKS, body, unroll)


def log_pass(operands, rows_ref, ratio_ref, part_ref, top_ref, head, margin, large, terms_ref=None):
    size = operands[0].shape[0]
    find_tops(min(head, size), operands, rows_ref, top_ref)
    top_ref[...] = top_ref[...] + margin
    sum_pass(operands, rows_ref, -top_ref[...], ratio_ref, part_ref, terms_ref)

    @pl.when(jnp.logical_not(jnp.max(part_ref[...]) < large))
    def _():
        find_tops(size, operands, rows_ref, top_ref, unroll=False)
        sum_pass(operands, rows_ref, -top_ref[...], ratio_ref, part_ref, terms_ref, unroll=False)


def product_pass(terms_ref, factor, rows_ref, part_ref):
    spread(factor, rows_ref)
    size = terms_ref.shape[1]

    def step(g, total):
        for q in range(GROUPS):
            at = pl.ds(pl.multiple_of((g * GROUPS + q) * 8, 8), 8)
            total = total + terms_ref[at, :] * jnp.concatenate([rows_ref[at, :]] * (size // LANES), axis=1)
        return total

    total = lax.fori_loop(0, terms_ref.shape[0] // (8 * GROUPS), step, jnp.zeros((8, size), f32))
    total = jnp.sum(total, axis=0, keepdims=True)
    for b in range(size // LANES):
        part_ref[b : b + 1, :] = total[:, b * LANES : (b + 1) * LANES]


def combine_logs(got_ref, shift):
    got = got_ref[...]
    top = jnp.max(got, axis=0)
    return -(top + log2(jnp.sum(jnp.exp2(got - top[None]), axis=0))) - shift


def combine_sums(got_ref, total):
    return 1.0 / (total * jnp.sum(got_ref[...], axis=0))


def send(part, out_ref):
    out_ref[...] = jnp.broadcast_to(part[None], out_ref.shape)


def pack_kernel(src_embed, tgt_embed, src_weight, tgt_weight, src_out, tgt_out, embeds, weights, sems):
    copies = [
        pltpu.make_async_copy(source, target, sems.at[k])
        for k, (source, target) in enumerate(
            [
                (src_embed, embeds.at[0]),
                (tgt_embed, embeds.at[1]),
                (src_weight, weights.at[0]),
                (tgt_weight, weights.at[1]),
            ]
        )
    ]
    for copy in copies:
        copy.start()
    for copy in copies:
        copy.wait()
    for k, out in enumerate((src_out, tgt_out)):
        row = jnp.broadcast_to(weights[k].astype(f32), (PACK, LANES)).astype(bf16)
        send(jnp.concatenate([embeds[k], row], axis=0), out)


def sources_kernel(own, far, _, wide, tail, raw, scale):
    x, y, core = lax.axis_index("x"), lax.axis_index("y"), lax.axis_index("c")
    blocks = []
    for m in range(4):
        for k in range(4):
            ref = own.at[k] if m == 0 else far.at[m - 1, k]
            dx, dy = jnp.where(core == 0, k, m), jnp.where(core == 0, m, k)
            blocks.append((ref, (x ^ dx) * 4 + (y ^ dy)))
    prepare(blocks, wide, tail, raw, scale)


def targets_kernel(own, other, wide, tail, raw, scale):
    core = lax.axis_index("c")
    blocks = [(own.at[z], 2 * z + core) for z in range(own.shape[0])]
    blocks += [(other.at[z], 2 * z + 1 - core) for z in range(own.shape[0])]
    prepare(blocks, wide, tail, raw, scale)


def first_kernel(wide, raw, tail, scale, out, ratio, part, top):
    log_pass((wide, raw, tail, scale), None, ratio, part, top, 512, 100.0, 2.0**120)
    send(top[...] + log2(part[...]), out)


def second_kernel(shift, got, wide, raw, tail, scale, new, part, lse, terms, out, rows, ratio, top):
    new[...] = combine_logs(got, shift)
    spread(new[...], rows)
    log_pass((wide, raw, tail, scale), rows, ratio, part, top, 128, 30.0, 2.0**80, terms)
    lse[...] = top[...] + log2(part[...])
    send(lse[...], out)


def third_kernel(shift, got, kept, lse, mass, wide, raw, tail, scale, new, terms, weight, one, out, rows, ratio, part):
    new[...] = combine_logs(got, shift)
    weight[...] = jnp.exp2(lse[...] + new[...]) / mass[...]
    one[...] = jnp.ones_like(one)
    spread(new[...], rows)
    sum_pass((wide, raw, tail, scale), rows, kept[...], ratio, part, terms)
    send(part[...], out)


def product_kernel(total, got, terms, weight, out, rows, part, factor):
    factor[...] = combine_sums(got, total)
    product_pass(terms, factor[...], rows, part)
    send(part[...] * weight[...], out)


def last_product_kernel(total, got, terms, weight, factor, out, rows, part):
    product_kernel(total, got, terms, weight, out, rows, part, factor)


def last_kernel(total, got, f, g, f_factor, g_factor, out, own_src, own_tgt):
    diff = jnp.log(f_factor[...] * (total * jnp.sum(got[...], axis=0)))
    out[...] = jnp.full(out.shape, jnp.sum(diff * diff), f32)
    at = pl.ds(lax.axis_index(SRC_GROUP), 1)
    own_src[...] = (f[at, :] + log2(f_factor[at, :])) * (1.0 / UNIT)
    at = pl.ds(lax.axis_index(TGT_GROUP), 1)
    own_tgt[...] = (g[at, :] + log2(g_factor[at, :])) * (1.0 / UNIT)


def call(kernel, args, outs, scratch, name):
    return pl.pallas_call(
        kernel,
        out_shape=[jax.ShapeDtypeStruct(shape, dtype) for shape, dtype in outs],
        in_specs=[pl.BlockSpec(memory_space=pltpu.VMEM)] * len(args),
        out_specs=[pl.BlockSpec(memory_space=pltpu.VMEM)] * len(outs),
        scratch_shapes=scratch,
        compiler_params=pltpu.CompilerParams(vmem_limit_bytes=VMEM),
        name=name,
    )(*args)


def exchange(sent, group):
    return lax.all_to_all(sent, group, 0, 0)


def crossed(array, turn):
    out = []
    for k in range(1, 4):
        pairs = []
        for x in range(4):
            for y in range(4):
                for core in range(2):
                    other = (x ^ k, y) if core == turn else (x, y ^ k)
                    pairs.append(((x * 4 + y) * 2 + core, (other[0] * 4 + other[1]) * 2 + core))
        out.append(lax.ppermute(array, ("x", "y", "c"), pairs))
    return out


def on_device(src_embed, tgt_embed, src_weight, tgt_weight):
    depth, per_dev = src_embed.shape
    src_count, tgt_count = lax.axis_size(SRC_GROUP), lax.axis_size(TGT_GROUP)
    total = per_dev * src_count * tgt_count
    shift = math.log2(total)
    src_size, tgt_size = per_dev * src_count, per_dev * tgt_count
    src_rows, tgt_rows = (src_count, per_dev), (tgt_count, per_dev)

    cells = (depth + PACK, per_dev)
    z_count = tgt_count // lax.axis_size("c")
    src_sent, tgt_sent = pl.pallas_call(
        pack_kernel,
        out_shape=[
            pltpu.VMEM((1,) + cells, bf16),
            pltpu.VMEM((z_count,) + cells, bf16),
        ],
        in_specs=[pl.BlockSpec(memory_space=pl.ANY)] * 4,
        out_specs=[pl.BlockSpec(memory_space=pltpu.VMEM)] * 2,
        scratch_shapes=[
            pltpu.VMEM((2, depth, per_dev), bf16),
            pltpu.VMEM((2, 1, per_dev), bf16),
            pltpu.SemaphoreType.DMA((4,)),
        ],
        name="pack",
    )(src_embed, tgt_embed, src_weight[None], tgt_weight[None])

    def neighbours(array, axis):
        size = lax.axis_size(axis)
        return [lax.ppermute(array, axis, [(i, i ^ k) for i in range(size)]) for k in range(1, size)]

    tgt = exchange(tgt_sent, ("zh", "zl"))
    src = jnp.concatenate([src_sent] + crossed(src_sent, 0), axis=0)
    src_far = jnp.stack(crossed(src, 1))
    (tgt_other,) = neighbours(tgt, "c")

    wide = 2 * depth + TAIL

    def operands(size, rows):
        return [((size, wide), bf16), ((TAIL, size), f32), ((depth, size), bf16), (rows, f32)]

    row_out = ((src_count,) + src_rows, f32)
    col_out = ((tgt_count,) + tgt_rows, f32)
    row_part = pltpu.VMEM(src_rows, f32)
    col_part = pltpu.VMEM(tgt_rows, f32)
    row_ratio = pltpu.VMEM((3,) + src_rows, f32)
    col_ratio = pltpu.VMEM((3,) + tgt_rows, f32)

    t_wide, t_tail, t_raw, t_scale = call(
        targets_kernel, [tgt, tgt_other], operands(tgt_size, tgt_rows), [], "targets"
    )
    s_wide, s_tail, s_raw, s_scale = call(
        sources_kernel, [src, src_far, t_scale], operands(src_size, src_rows), [], "sources"
    )
    (sent,) = call(
        first_kernel,
        [t_wide, s_raw, s_tail, s_scale],
        [row_out],
        [row_ratio, row_part, row_part],
        "row_pass_1",
    )
    got = exchange(sent, SRC_GROUP)
    src_spread = pltpu.VMEM((src_size, LANES), f32)
    tgt_spread = pltpu.VMEM((tgt_size, LANES), f32)
    keep_tgt = [t_raw, t_tail, t_scale]
    keep_src = [s_raw, s_tail, s_scale]

    f, part, lse, terms, sent = call(
        functools.partial(second_kernel, shift),
        [got, s_wide] + keep_tgt,
        [(src_rows, f32), (tgt_rows, f32), (tgt_rows, f32), ((src_size, tgt_size), f32), col_out],
        [src_spread, col_ratio, col_part],
        "col_pass_1",
    )
    got = exchange(sent, TGT_GROUP)
    g, mate, weight, one, sent = call(
        functools.partial(third_kernel, shift),
        [got, f, lse, part, t_wide] + keep_src,
        [(tgt_rows, f32), ((tgt_size, src_size), f32), (tgt_rows, f32), (src_rows, f32), row_out],
        [tgt_spread, row_ratio, row_part],
        "row_pass_2",
    )
    def product(got, terms, weight, rows, out, spread_rows, part, last):
        args, kept = [got, terms, weight], (rows, f32)
        if not last:
            kernel = functools.partial(product_kernel, float(total))
            return None, call(kernel, args, [out], [spread_rows, part, pltpu.VMEM(*kept)], "product")[0]
        kernel = functools.partial(last_product_kernel, float(total))
        return call(kernel, args, [kept, out], [spread_rows, part], "last_product")

    for step in range(2, ITERS + 1):
        last = step == ITERS
        got = exchange(sent, SRC_GROUP)
        f_factor, sent = product(got, terms, weight, src_rows, col_out, src_spread, col_part, last)
        got = exchange(sent, TGT_GROUP)
        g_factor, sent = product(got, mate, one, tgt_rows, row_out, tgt_spread, row_part, last)
    got = exchange(sent, SRC_GROUP)
    sent, own_src, own_tgt = call(
        functools.partial(last_kernel, float(total)),
        [got, f, g, f_factor, g_factor],
        [((tgt_count, 1, LANES), f32), ((1, per_dev), f32), ((1, per_dev), f32)],
        [],
        "mismatch",
    )
    squares = jnp.sum(exchange(sent, TGT_GROUP)[:, 0, 0])
    return own_src[0], own_tgt[0], jnp.sqrt(squares / total)


def solution(mesh, shape=(4, 4, 2, 4, 2)):
    placed = Mesh(mesh.devices.reshape(shape), AXES)
    return jax.shard_map(
        on_device,
        mesh=placed,
        in_specs=(P(None, AXES), P(None, AXES), P(AXES), P(AXES)),
        out_specs=(P(AXES), P(AXES), P()),
        check_vma=False,
    )
```

```python
import functools
import math

import jax
import jax.numpy as jnp
from jax import lax
from jax.experimental import pallas as pl
from jax.experimental.pallas import tpu as pltpu
from jax.sharding import Mesh, PartitionSpec as P

EPS = 0.02
ITERS = 3
LANES = 128
TAIL = 16
PACK = 16
BLOCKS = 2
WIDTH = BLOCKS * LANES
GROUPS = 128
VMEM = 8 * 1024 * 1024
UNIT = 1.0 / (EPS * math.log(2.0))
AXES = ("x", "zh", "zl", "y", "c")
SRC_GROUP = ("x", "y")
TGT_GROUP = ("zh", "zl", "c")

f32 = jnp.float32
bf16 = jnp.bfloat16


def log2(value):
    return jnp.log(value) * (1.0 / math.log(2.0))


def pieces(value):
    high = value.astype(bf16).astype(f32)
    rest = value - high
    middle = rest.astype(bf16).astype(f32)
    low = (rest - middle).astype(bf16).astype(f32)
    return high, middle, low


def stack(rows, width):
    index = lax.broadcasted_iota(jnp.int32, (TAIL, width), 0)
    out = jnp.zeros((TAIL, width), f32)
    for place, row in rows:
        out = jnp.where(index == place, row, out)
    return out


def prepare(blocks, wide_ref, tail_ref, raw_ref, scale_ref):
    depth = raw_ref.shape[0]
    for cells, place in blocks:
        at = pl.ds(pl.multiple_of(place * LANES, LANES), LANES)
        embed = cells[:depth, :]
        raw_ref[:, at] = embed
        value = embed.astype(f32)
        weight = cells[depth : depth + PACK, :].astype(f32)[0:1]
        norm = jnp.sum(value * value, axis=0, keepdims=True)
        scale_ref[pl.ds(place, 1), :] = weight * (UNIT / depth)
        scaled = (2.0 * weight) * value
        high = scaled.astype(bf16).astype(f32)
        low = scaled - high
        one = jnp.ones_like(weight)
        n = pieces(norm)
        wn = pieces(weight * norm)
        tail_ref[:, at] = stack([(0, one), (1, one), (2, one), (3, n[0]), (4, n[1]), (5, n[2])], LANES)
        tail = stack(
            [(0, -wn[0]), (1, -wn[1]), (2, -wn[2])]
            + [(3, -weight), (4, -weight), (5, -weight), (6, one), (7, one), (8, one)],
            LANES,
        )
        wide_ref[at, :] = jnp.concatenate([high, low, tail], axis=0).T.astype(bf16)


def spread(summed, rows_ref):
    column = summed.T
    for b in range(rows_ref.shape[0] // LANES):
        rows_ref[pl.ds(b * LANES, LANES), :] = jnp.broadcast_to(column[:, b : b + 1], (LANES, LANES))


def strip_of(s):
    return pl.ds(s * WIDTH, WIDTH) if isinstance(s, int) else pl.ds(pl.multiple_of(s * WIDTH, WIDTH), WIDTH)


def get(ref, s):
    return jnp.concatenate([ref[pl.ds(BLOCKS * s + k, 1), :] for k in range(BLOCKS)], axis=1)


def put(ref, s, value):
    for k in range(BLOCKS):
        ref[pl.ds(BLOCKS * s + k, 1), :] = value[:, k * LANES : (k + 1) * LANES]


def strip_score(s, count, operands, rows_ref, ratio_ref):
    wide_ref, raw_ref, tail_ref, scale_ref = operands
    at = strip_of(s)
    tail = tail_ref[:, at]
    if ratio_ref is not None:
        tail = tail + stack([(6 + k, get(ratio_ref.at[k], s)) for k in range(3)], WIDTH)
    raw = raw_ref[:, at]
    operand = jnp.concatenate([raw, raw, tail.astype(bf16)], axis=0)
    score = jnp.dot(wide_ref[:count, :], operand, preferred_element_type=f32) * get(scale_ref, s)
    if rows_ref is not None:
        rows = rows_ref[:count, :]
        score = score + jnp.concatenate([rows] * BLOCKS, axis=1)
    return score


def strips(count, body, unroll):
    if unroll:
        for s in range(count):
            body(s)
    else:

        def step(s, carry):
            body(s)
            return carry

        lax.fori_loop(0, count, step, 0)


def find_tops(count, operands, rows_ref, top_ref, unroll=True):
    def body(s):
        put(top_ref, s, jnp.max(strip_score(s, count, operands, rows_ref, None), axis=0, keepdims=True))

    strips(top_ref.shape[0] // BLOCKS, body, unroll)


def sum_pass(operands, rows_ref, kept, ratio_ref, part_ref, terms_ref=None, unroll=True):
    for k, piece in enumerate(pieces(kept / operands[3][...])):
        ratio_ref[k] = piece

    def body(s):
        terms = jnp.exp2(strip_score(s, operands[0].shape[0], operands, rows_ref, ratio_ref))
        if terms_ref is not None:
            terms_ref[:, strip_of(s)] = terms
        put(part_ref, s, jnp.sum(terms, axis=0, keepdims=True))

    strips(part_ref.shape[0] // BLOCKS, body, unroll)


def log_pass(operands, rows_ref, ratio_ref, part_ref, top_ref, head, margin, large, terms_ref=None):
    size = operands[0].shape[0]
    find_tops(min(head, size), operands, rows_ref, top_ref)
    top_ref[...] = top_ref[...] + margin
    sum_pass(operands, rows_ref, -top_ref[...], ratio_ref, part_ref, terms_ref)

    @pl.when(jnp.logical_not(jnp.max(part_ref[...]) < large))
    def _():
        find_tops(size, operands, rows_ref, top_ref, unroll=False)
        sum_pass(operands, rows_ref, -top_ref[...], ratio_ref, part_ref, terms_ref, unroll=False)


def product_pass(terms_ref, factor, rows_ref, part_ref):
    spread(factor, rows_ref)
    size = terms_ref.shape[1]

    def step(g, total):
        for q in range(GROUPS):
            at = pl.ds(pl.multiple_of((g * GROUPS + q) * 8, 8), 8)
            total = total + terms_ref[at, :] * jnp.concatenate([rows_ref[at, :]] * (size // LANES), axis=1)
        return total

    total = lax.fori_loop(0, terms_ref.shape[0] // (8 * GROUPS), step, jnp.zeros((8, size), f32))
    total = jnp.sum(total, axis=0, keepdims=True)
    for b in range(size // LANES):
        part_ref[b : b + 1, :] = total[:, b * LANES : (b + 1) * LANES]


def combine_logs(got_ref, shift):
    got = got_ref[...]
    top = jnp.max(got, axis=0)
    return -(top + log2(jnp.sum(jnp.exp2(got - top[None]), axis=0))) - shift


def combine_sums(got_ref, total):
    return 1.0 / (total * jnp.sum(got_ref[...], axis=0))


def send(part, out_ref):
    out_ref[...] = jnp.broadcast_to(part[None], out_ref.shape)


def pack_kernel(src_embed, tgt_embed, src_weight, tgt_weight, src_out, tgt_out, embeds, weights, sems):
    copies = [
        pltpu.make_async_copy(source, target, sems.at[k])
        for k, (source, target) in enumerate(
            [
                (src_embed, embeds.at[0]),
                (tgt_embed, embeds.at[1]),
                (src_weight, weights.at[0]),
                (tgt_weight, weights.at[1]),
            ]
        )
    ]
    for copy in copies:
        copy.start()
    for copy in copies:
        copy.wait()
    for k, out in enumerate((src_out, tgt_out)):
        row = jnp.broadcast_to(weights[k].astype(f32), (PACK, LANES)).astype(bf16)
        send(jnp.concatenate([embeds[k], row], axis=0), out)


def sources_kernel(own, far, _, wide, tail, raw, scale):
    x, y = lax.axis_index("x"), lax.axis_index("y")
    blocks = []
    for m in range(4):
        for k in range(4):
            ref = (own.at[k] if m == 0 else far.at[m - 1, k])
            blocks.append((ref, (x ^ k) * 4 + (y ^ m)))
    prepare(blocks, wide, tail, raw, scale)


def targets_kernel(own, other, wide, tail, raw, scale):
    core = lax.axis_index("c")
    blocks = [(own.at[z], 2 * z + core) for z in range(own.shape[0])]
    blocks += [(other.at[z], 2 * z + 1 - core) for z in range(own.shape[0])]
    prepare(blocks, wide, tail, raw, scale)


def first_kernel(wide, raw, tail, scale, out, ratio, part, top):
    log_pass((wide, raw, tail, scale), None, ratio, part, top, 512, 100.0, 2.0**120)
    send(top[...] + log2(part[...]), out)


def second_kernel(shift, got, wide, raw, tail, scale, new, part, lse, terms, out, rows, ratio, top):
    new[...] = combine_logs(got, shift)
    spread(new[...], rows)
    log_pass((wide, raw, tail, scale), rows, ratio, part, top, 128, 30.0, 2.0**80, terms)
    lse[...] = top[...] + log2(part[...])
    send(lse[...], out)


def third_kernel(shift, got, kept, lse, mass, wide, raw, tail, scale, new, terms, weight, one, out, rows, ratio, part):
    new[...] = combine_logs(got, shift)
    weight[...] = jnp.exp2(lse[...] + new[...]) / mass[...]
    one[...] = jnp.ones_like(one)
    spread(new[...], rows)
    sum_pass((wide, raw, tail, scale), rows, kept[...], ratio, part, terms)
    send(part[...], out)


def product_kernel(total, got, terms, weight, out, rows, part, factor):
    factor[...] = combine_sums(got, total)
    product_pass(terms, factor[...], rows, part)
    send(part[...] * weight[...], out)


def last_product_kernel(total, got, terms, weight, factor, out, rows, part):
    product_kernel(total, got, terms, weight, out, rows, part, factor)


def last_kernel(total, got, f, g, f_factor, g_factor, out, own_src, own_tgt):
    diff = jnp.log(f_factor[...] * (total * jnp.sum(got[...], axis=0)))
    out[...] = jnp.full(out.shape, jnp.sum(diff * diff), f32)
    at = pl.ds(lax.axis_index(SRC_GROUP), 1)
    own_src[...] = (f[at, :] + log2(f_factor[at, :])) * (1.0 / UNIT)
    at = pl.ds(lax.axis_index(TGT_GROUP), 1)
    own_tgt[...] = (g[at, :] + log2(g_factor[at, :])) * (1.0 / UNIT)


def call(kernel, args, outs, scratch, name):
    return pl.pallas_call(
        kernel,
        out_shape=[jax.ShapeDtypeStruct(shape, dtype) for shape, dtype in outs],
        in_specs=[pl.BlockSpec(memory_space=pltpu.VMEM)] * len(args),
        out_specs=[pl.BlockSpec(memory_space=pltpu.VMEM)] * len(outs),
        scratch_shapes=scratch,
        compiler_params=pltpu.CompilerParams(vmem_limit_bytes=VMEM),
        name=name,
    )(*args)


def exchange(sent, group):
    return lax.all_to_all(sent, group, 0, 0)


def on_device(src_embed, tgt_embed, src_weight, tgt_weight):
    depth, per_dev = src_embed.shape
    src_count, tgt_count = lax.axis_size(SRC_GROUP), lax.axis_size(TGT_GROUP)
    total = per_dev * src_count * tgt_count
    shift = math.log2(total)
    src_size, tgt_size = per_dev * src_count, per_dev * tgt_count
    src_rows, tgt_rows = (src_count, per_dev), (tgt_count, per_dev)

    cells = (depth + PACK, per_dev)
    z_count = tgt_count // lax.axis_size("c")
    src_sent, tgt_sent = pl.pallas_call(
        pack_kernel,
        out_shape=[
            pltpu.VMEM((1,) + cells, bf16),
            pltpu.VMEM((z_count,) + cells, bf16),
        ],
        in_specs=[pl.BlockSpec(memory_space=pl.ANY)] * 4,
        out_specs=[pl.BlockSpec(memory_space=pltpu.VMEM)] * 2,
        scratch_shapes=[
            pltpu.VMEM((2, depth, per_dev), bf16),
            pltpu.VMEM((2, 1, per_dev), bf16),
            pltpu.SemaphoreType.DMA((4,)),
        ],
        name="pack",
    )(src_embed, tgt_embed, src_weight[None], tgt_weight[None])

    def neighbours(array, axis):
        size = lax.axis_size(axis)
        return [lax.ppermute(array, axis, [(i, i ^ k) for i in range(size)]) for k in range(1, size)]

    tgt = exchange(tgt_sent, ("zh", "zl"))
    src = jnp.concatenate([src_sent] + neighbours(src_sent, "x"), axis=0)
    src_far = jnp.stack(neighbours(src, "y"))
    (tgt_other,) = neighbours(tgt, "c")

    wide = 2 * depth + TAIL

    def operands(size, rows):
        return [((size, wide), bf16), ((TAIL, size), f32), ((depth, size), bf16), (rows, f32)]

    row_out = ((src_count,) + src_rows, f32)
    col_out = ((tgt_count,) + tgt_rows, f32)
    row_part = pltpu.VMEM(src_rows, f32)
    col_part = pltpu.VMEM(tgt_rows, f32)
    row_ratio = pltpu.VMEM((3,) + src_rows, f32)
    col_ratio = pltpu.VMEM((3,) + tgt_rows, f32)

    t_wide, t_tail, t_raw, t_scale = call(
        targets_kernel, [tgt, tgt_other], operands(tgt_size, tgt_rows), [], "targets"
    )
    s_wide, s_tail, s_raw, s_scale = call(
        sources_kernel, [src, src_far, t_scale], operands(src_size, src_rows), [], "sources"
    )
    (sent,) = call(
        first_kernel,
        [t_wide, s_raw, s_tail, s_scale],
        [row_out],
        [row_ratio, row_part, row_part],
        "row_pass_1",
    )
    got = exchange(sent, SRC_GROUP)
    src_spread = pltpu.VMEM((src_size, LANES), f32)
    tgt_spread = pltpu.VMEM((tgt_size, LANES), f32)
    keep_tgt = [t_raw, t_tail, t_scale]
    keep_src = [s_raw, s_tail, s_scale]

    f, part, lse, terms, sent = call(
        functools.partial(second_kernel, shift),
        [got, s_wide] + keep_tgt,
        [(src_rows, f32), (tgt_rows, f32), (tgt_rows, f32), ((src_size, tgt_size), f32), col_out],
        [src_spread, col_ratio, col_part],
        "col_pass_1",
    )
    got = exchange(sent, TGT_GROUP)
    g, mate, weight, one, sent = call(
        functools.partial(third_kernel, shift),
        [got, f, lse, part, t_wide] + keep_src,
        [(tgt_rows, f32), ((tgt_size, src_size), f32), (tgt_rows, f32), (src_rows, f32), row_out],
        [tgt_spread, row_ratio, row_part],
        "row_pass_2",
    )
    def product(got, terms, weight, rows, out, spread_rows, part, last):
        args, kept = [got, terms, weight], (rows, f32)
        if not last:
            kernel = functools.partial(product_kernel, float(total))
            return None, call(kernel, args, [out], [spread_rows, part, pltpu.VMEM(*kept)], "product")[0]
        kernel = functools.partial(last_product_kernel, float(total))
        return call(kernel, args, [kept, out], [spread_rows, part], "last_product")

    for step in range(2, ITERS + 1):
        last = step == ITERS
        got = exchange(sent, SRC_GROUP)
        f_factor, sent = product(got, terms, weight, src_rows, col_out, src_spread, col_part, last)
        got = exchange(sent, TGT_GROUP)
        g_factor, sent = product(got, mate, one, tgt_rows, row_out, tgt_spread, row_part, last)
    got = exchange(sent, SRC_GROUP)
    sent, own_src, own_tgt = call(
        functools.partial(last_kernel, float(total)),
        [got, f, g, f_factor, g_factor],
        [((tgt_count, 1, LANES), f32), ((1, per_dev), f32), ((1, per_dev), f32)],
        [],
        "mismatch",
    )
    squares = jnp.sum(exchange(sent, TGT_GROUP)[:, 0, 0])
    return own_src[0], own_tgt[0], jnp.sqrt(squares / total)


def solution(mesh, shape=(4, 4, 2, 4, 2)):
    placed = Mesh(mesh.devices.reshape(shape), AXES)
    return jax.shard_map(
        on_device,
        mesh=placed,
        in_specs=(P(None, AXES), P(None, AXES), P(AXES), P(AXES)),
        out_specs=(P(AXES), P(AXES), P()),
        check_vma=False,
    )
```
